128 devices in a mesh: lon: 16 (over y_lo, x, core), sub: 8 (over z, y_hi).
Axes of the slice: x: 4, y: 4 (y_hi: 2, y_lo: 2; y = y_hi * 2 + y_lo), z: 4, core: 2. Of those that a mesh axis runs over, the one named last changes fastest.
Arguments:
- atm_tracer: float32 [128, 128, 4096], P('sub', None, 'lon'), may hold values from -6 to 6
- courant: float32 [128, 128, 4096], P('sub', None, 'lon'), may hold values from -0.9 to 0.9
- column_inverse: float32 [8, 128, 128], replicated
- heat_exchange_factor: float32 [128, 4096], P(None, 'lon'), may hold values from 0.3 to 3
- ocean_temp: float32 [32, 64, 2048], P(None, 'sub', 'lon'), may hold values from -6 to 6
- diffusivity: float32 [64, 2048], P('sub', 'lon'), may hold values from 0.04 to 0.2
- ocean_inverse: float32 [32, 32], replicated
- land_mask: int32 [64, 2048], P('sub', 'lon'), may hold values 0 or 1
- regrid_weight_blocks: float32 [64, 128, 128], replicated, may hold values from -0.25 to 0.25
- a2o_src: int32 [64, 16, 4], P('sub', 'lon'), may hold values from 0 to 4095, as said below
- a2o_wgt: int32 [64, 16, 4], P('sub', 'lon'), may hold values from 0 to 63
- ocean_to_atmos_source: int32 [128, 32, 4], P(None, 'lon'), may hold values from 0 to 1023, as said below
- ocean_to_atmos_weight: int32 [128, 32, 4], P(None, 'lon'), may hold values from 0 to 63
Outputs:
- atmos_temp_updated: float32 [128, 128, 4096], P('sub', None, 'lon')
- ocean_new: float32 [32, 64, 2048], P(None, 'sub', 'lon')
- atmos_heat_flux: float32 [128, 4096], P('sub', 'lon')
The draws below stay inside these ranges and needn't reach their ends.
Inputs may be any that keep to these rules, and one draw needn't show every extreme that they name: `a2o_src`: for ocean block row r in tile column t, every entry names an atmosphere block of a row in r // 8 * 16 to (r // 8 + 1) * 16 - 1 and of a column group g with (g - t * 2) mod 32 below 4. `ocean_to_atmos_source`: for atmosphere block row r and column group g, every entry names an ocean block of a row in r // 16 * 8 to (r // 16 + 1) * 8 - 1 and of tile column s or s - 1 (mod 16), where s = g // 2.
All inputs are finite; a program needn't handle non-finite values. No bound on the sum of `land_mask` on one device may be relied on, other than what follows from the above.
Results may differ from the reference program's by a relative error of at most 0.000096.
Values sent between devices are 32-bit elements; how exact they have to be, the bound alone decides.
No kernel may reach another device: no remote copies, remote signals or barrier semaphores. Data moves between devices by JAX's collectives and lax.ppermute only.
A program may use at most 64 MiB of HBM per device.

```python
import math
import jax
import jax.numpy as jnp
from jax import lax

ATMOS_LEVELS = 128
ATMOS_LAT_ROWS = 128
ALON_DEV = 256
OLON_DEV = 128
OLAT_DEV = 8
OLEV = 32
NBAND = 8
INTERSECT_COUNT = 4
NW = 64
TILES = 16
ATMOS_LON_CELLS = 4096
OLAT = 64
OLON = 2048
NG = 32
ABAND = 16


def square_inverse(key, count, order):
    key_diag, key_off = jax.random.split(key, 2)
    diag = jax.random.uniform(key_diag, (count, order), minval=0.6, maxval=1.4)
    offdiag = jax.random.normal(key_off, (count, order, order)) * (0.5 / math.sqrt(order))
    matrix = offdiag + diag[:, :, None] * jnp.eye(order, dtype=jnp.float32)[None]
    return matrix.astype(jnp.float32)


def draw_column_inverse(key, part):
    return square_inverse(jax.random.fold_in(key, 11), NBAND, ATMOS_LEVELS)


def draw_ocean_inverse(key, part):
    return square_inverse(jax.random.fold_in(key, 12), 1, OLEV)[0]


def draw_a2o_src(key, part):
    key_row, key_grp = jax.random.split(jax.random.fold_in(key, 21))
    groups = ALON_DEV // OLON_DEV
    rows = jnp.arange(OLAT, dtype=jnp.int32)[:, None, None]
    tiles = jnp.arange(TILES, dtype=jnp.int32)[None, :, None]
    atm_row = rows // OLAT_DEV * ABAND + jax.random.randint(key_row, (OLAT, TILES, INTERSECT_COUNT), 0, ABAND)
    atm_grp = (tiles * groups + jax.random.randint(key_grp, (OLAT, TILES, INTERSECT_COUNT), 0, 2 * groups)) % NG
    return (atm_row * NG + atm_grp).astype(jnp.int32)


def draw_ocean_to_atmos_source(key, part):
    key_row, key_tile = jax.random.split(jax.random.fold_in(key, 31))
    groups = ALON_DEV // OLON_DEV
    rows = jnp.arange(ATMOS_LAT_ROWS, dtype=jnp.int32)[:, None, None]
    grps = jnp.arange(NG, dtype=jnp.int32)[None, :, None]
    ocean_row = rows // ABAND * OLAT_DEV + jax.random.randint(key_row, (ATMOS_LAT_ROWS, NG, INTERSECT_COUNT), 0, OLAT_DEV)
    ocean_tile = (grps // groups - jax.random.randint(key_tile, (ATMOS_LAT_ROWS, NG, INTERSECT_COUNT), 0, 2)) % TILES
    return (ocean_row * TILES + ocean_tile).astype(jnp.int32)


def with_ends(values, stream_key, least, high):
    index_at = [jax.random.randint(jax.random.fold_in(stream_key, axis), (), 0, length) for axis, length in enumerate(values.shape)]
    main_axis = values.shape.index(max(values.shape))
    next_to = index_at[:main_axis] + [(index_at[main_axis] + 1) % values.shape[main_axis]] + index_at[main_axis + 1:]
    return values.at[tuple(index_at)].set(least).at[tuple(next_to)].set(high)


def block_levels(stream_key, shape, cuts, least, top_value):
    def one(position, blocks):
        heights = jax.random.uniform(jax.random.fold_in(jax.random.fold_in(stream_key, 6), position), (blocks,), jnp.float32, least / len(cuts), top_value / len(cuts))
        return jnp.repeat(jnp.exp(heights), shape[position] // blocks).reshape((-1,) + (1,) * (len(shape) - position - 1))

    loudness = one(*cuts[0])
    for cut in cuts[1:]:
        loudness = loudness * one(*cut)
    return loudness


def scatter_about(own_key, extent, scale, reach, cuts=(), kind=jnp.bfloat16):
    drawn = scale * jax.random.normal(own_key, extent, jnp.float32)
    if cuts:
        drawn = drawn * block_levels(own_key, extent, cuts, -0.22, 0.18)
    return jnp.clip(drawn, -reach, reach).astype(kind)


def setup_inputs(seed: int = 0) -> dict:
    keys = jax.random.split(jax.random.key(seed), 14)
    return {
        "atm_tracer": scatter_about(keys[0], (ATMOS_LEVELS, ATMOS_LAT_ROWS, ATMOS_LON_CELLS), 1.0, 6.0, ((0, 8), (2, 16)), jnp.float32),
        "courant": jnp.clip(jax.random.uniform(keys[1], (ATMOS_LEVELS, ATMOS_LAT_ROWS, ATMOS_LON_CELLS), jnp.float32, -0.9, 0.9) * block_levels(keys[1], (ATMOS_LEVELS, ATMOS_LAT_ROWS, ATMOS_LON_CELLS), ((0, 8), (2, 16)), -0.4, 0.0), -0.9, 0.9),
        "column_inverse": draw_column_inverse(jax.random.fold_in(keys[13], 71), 0),
        "heat_exchange_factor": jnp.clip(jnp.exp(math.log(3.0) - 2.3025851 * jax.random.uniform(keys[3], (ATMOS_LAT_ROWS, ATMOS_LON_CELLS), jnp.float32) ** block_levels(keys[3], (ATMOS_LAT_ROWS, ATMOS_LON_CELLS), ((1, 16),), -0.2, 0.2)), 0.3, 3.0),
        "ocean_temp": scatter_about(keys[4], (OLEV, OLAT, OLON), 1.0, 6.0, ((1, 8), (2, 16)), jnp.float32),
        "diffusivity": jnp.clip(0.04 + 0.16 * jax.random.uniform(keys[5], (OLAT, OLON), jnp.float32) ** block_levels(keys[5], (OLAT, OLON), ((0, 8), (1, 16)), -0.2, 0.2), 0.04, 0.2),
        "ocean_inverse": draw_ocean_inverse(jax.random.fold_in(keys[13], 71), 0),
        "land_mask": with_ends((jax.random.randint(keys[7], (OLAT, OLON), 0, 4) < 3).astype(jnp.int32), jax.random.fold_in(keys[7], 1), 0, 1),
        "regrid_weight_blocks": scatter_about(keys[8], (NW, OLON_DEV, OLON_DEV), (OLON_DEV * INTERSECT_COUNT) ** -0.5, 0.25, (), jnp.float32),
        "a2o_src": draw_a2o_src(jax.random.fold_in(keys[13], 71), 0),
        "a2o_wgt": with_ends(jax.random.randint(keys[10], (OLAT, TILES, INTERSECT_COUNT), 0, NW), jax.random.fold_in(keys[10], 1), 0, NW - 1).astype(jnp.int32),
        "ocean_to_atmos_source": draw_ocean_to_atmos_source(jax.random.fold_in(keys[13], 71), 0),
        "ocean_to_atmos_weight": with_ends(jax.random.randint(keys[12], (ATMOS_LAT_ROWS, NG, INTERSECT_COUNT), 0, NW), jax.random.fold_in(keys[12], 1), 0, NW - 1).astype(jnp.int32),
    }


def regrid_block_list(blocks, src_ids, wgt_ids, weights):
    count = src_ids.shape[0]
    width = src_ids.shape[1]
    step = math.gcd(count, 16)

    def one_group(pair):
        src_part, wgt_part = pair
        picked = blocks[src_part]
        mats = weights[wgt_part]
        return jnp.einsum("dkij,dkj->di", mats, picked, precision=lax.Precision.HIGHEST)

    result = lax.map(one_group, (src_ids.reshape(count // step, step, width), wgt_ids.reshape(count // step, step, width)))
    return result.reshape(count, blocks.shape[1])


def reference(atm_tracer, courant, column_inverse, heat_exchange_factor, ocean_temp, diffusivity, ocean_inverse, land_mask, regrid_weight_blocks, a2o_src, a2o_wgt, ocean_to_atmos_source, ocean_to_atmos_weight):
    west = jnp.roll(atm_tracer, 1, axis=2)
    east = jnp.roll(atm_tracer, -1, axis=2)
    advected = atm_tracer - jnp.maximum(courant, 0.0) * (atm_tracer - west) - jnp.minimum(courant, 0.0) * (east - atm_tracer)
    rows_band = ATMOS_LAT_ROWS // NBAND
    banded = advected.reshape(ATMOS_LEVELS, NBAND, rows_band * ATMOS_LON_CELLS)
    atmos_temp_updated = jnp.einsum("blm,mbc->lbc", column_inverse, banded, precision=lax.Precision.HIGHEST).reshape(ATMOS_LEVELS, ATMOS_LAT_ROWS, ATMOS_LON_CELLS)
    sea_mask = land_mask.astype(jnp.float32)
    sea = sea_mask * ocean_temp[0]
    ocean_block_list = sea.reshape(OLAT * TILES, OLON_DEV)
    sea_surface_temp_atmos = regrid_block_list(ocean_block_list, ocean_to_atmos_source.reshape(-1, INTERSECT_COUNT), ocean_to_atmos_weight.reshape(-1, INTERSECT_COUNT), regrid_weight_blocks).reshape(ATMOS_LAT_ROWS, ATMOS_LON_CELLS)
    atmos_heat_flux = heat_exchange_factor * (sea_surface_temp_atmos - atmos_temp_updated[ATMOS_LEVELS - 1])
    flux_blocks = atmos_heat_flux.reshape(ATMOS_LAT_ROWS * NG, OLON_DEV)
    flux_ocean = regrid_block_list(flux_blocks, a2o_src.reshape(-1, INTERSECT_COUNT), a2o_wgt.reshape(-1, INTERSECT_COUNT), regrid_weight_blocks).reshape(OLAT, OLON)
    temp = ocean_temp
    o_west = jnp.roll(temp, 1, axis=2)
    o_east = jnp.roll(temp, -1, axis=2)
    folded = jnp.flip(temp[:, OLAT - 1, :], axis=1)
    north = jnp.concatenate([temp[:, 1:, :], folded[:, None, :]], axis=1)
    south = jnp.concatenate([temp[:, :1, :], temp[:, :-1, :]], axis=1)
    lap = o_west + o_east + north + south - 4.0 * temp
    stepped = sea_mask * (temp + diffusivity * lap)
    stepped = stepped.at[0].add(sea_mask * flux_ocean)
    ocean_new = jnp.einsum("lm,mc->lc", ocean_inverse, stepped.reshape(OLEV, OLAT * OLON), precision=lax.Precision.HIGHEST).reshape(OLEV, OLAT, OLON)
    return atmos_temp_updated, ocean_new, atmos_heat_flux
```

```python
import functools

import jax
import jax.numpy as jnp
from jax import lax
from jax.experimental import pallas as pl
from jax.experimental.pallas import tpu as pltpu
from jax.sharding import PartitionSpec as P

F32 = jnp.float32
BF16 = jnp.bfloat16
VMEM = pl.BlockSpec(memory_space=pltpu.VMEM)
SMEM = pl.BlockSpec(memory_space=pltpu.SMEM)
ANY = pl.BlockSpec(memory_space=pl.ANY)
MIB = 1 << 20
LANES = 128


def kernel_call(body, out_shape, in_specs, out_specs, scratch=(), flops=0, moved=0, limit=16, name=None):
    return pl.pallas_call(
        body,
        out_shape=out_shape,
        in_specs=in_specs,
        out_specs=out_specs,
        scratch_shapes=list(scratch),
        compiler_params=pltpu.CompilerParams(vmem_limit_bytes=limit * MIB),
        cost_estimate=pl.CostEstimate(flops=flops, bytes_accessed=moved, transcendentals=0),
        name=name,
    )


def shape(*dims):
    return jax.ShapeDtypeStruct(dims, F32)


def split(value):
    high = value.astype(BF16)
    return high, (value - high.astype(F32)).astype(BF16)


def edges_kernel(atm, ocean, mask, east_msg, west_msg):
    levels, rows, cells = atm.shape
    lane = lax.broadcasted_iota(jnp.int32, (LANES, LANES), 1)

    def gathered(atm_col, ocean_col):
        total = jnp.zeros((LANES, LANES), F32)
        for level in range(levels):
            total = jnp.where(lane == level, atm[level, :, atm_col : atm_col + 1], total)
        for part in range(2):
            column = ocean[part * LANES : (part + 1) * LANES, ocean_col : ocean_col + 1]
            total = jnp.where(lane == levels + part, column, total)
        return total.T

    east_msg[:24, :] = gathered(cells - 1, LANES - 1)[:24, :]
    east_msg[24:, :] = mask[...].astype(F32) * ocean[:8, :]
    west_msg[...] = gathered(0, 0)[:24, :]


def advect_kernel(atm, courant, from_west, from_east, out, west_cols, east_cols):
    levels, _, cells = atm.shape
    band = out.shape[1]
    west_cols[...] = from_west[...].T
    east_cols[...] = from_east[...].T
    lane = lax.broadcasted_iota(jnp.int32, (band, cells), 1)

    @pl.loop(0, out.shape[0])
    def _(dest):
        rows = pl.ds(pl.multiple_of(dest * band, band), band)
        made = []
        for level in range(levels):
            here = atm[level, rows, :]
            speed = courant[level, rows, :]
            west = jnp.where(lane == 0, west_cols[rows, level : level + 1], pltpu.roll(here, 1, 1))
            east = jnp.where(
                lane == cells - 1, east_cols[rows, level : level + 1], pltpu.roll(here, cells - 1, 1)
            )
            made.append(
                here
                - jnp.maximum(speed, 0.0) * (here - west)
                - jnp.minimum(speed, 0.0) * (east - here)
            )
        out[dest] = jnp.swapaxes(jnp.stack(made), 0, 1)


def mat_vec(ids, first, count, source, weights):
    total = jnp.zeros(weights.shape[1:], F32)
    half = ids.shape[0] // 2
    for k in range(count):
        block = source[pl.ds(ids[first + k], 1), :]
        total = total + weights[ids[half + first + k]] * block
    return jnp.sum(total.T, axis=0, keepdims=True)


def sst_kernel(width, ids, from_west, ocean, mask, weights, sst, window, halves):
    window[:8, :] = from_west[24:32, :]
    window[8:, :] = mask[...].astype(F32) * ocean[:8, :]
    rows = sst.shape[0]

    @pl.loop(0, rows)
    def _(row):
        for g in range(2):
            halves[g, pl.ds(row, 1), :] = mat_vec(ids, (row * 2 + g) * width, width, window, weights)

    for g in range(2):
        sst[:, g * LANES : (g + 1) * LANES] = halves[g]


def solve_kernel(place, columns, inverse, factor, sst, out, flux, held):
    sub = place[0]
    groups, band, depth, cells = columns.shape
    levels = groups * depth
    high, low = split(inverse[sub])
    twice = jnp.concatenate([high, high], axis=1)

    @pl.loop(0, band)
    def _(row):
        here = columns[:, row].reshape(levels, cells)
        x_high, x_low = split(here)
        made = jnp.dot(
            twice, jnp.concatenate([x_high, x_low], axis=0), preferred_element_type=F32
        ) + jnp.dot(low, x_high, preferred_element_type=F32)
        held[row] = made

    for group in range(groups):
        out[group] = jnp.swapaxes(held[:, group * depth : (group + 1) * depth, :], 0, 1)
    rows = pl.ds(pl.multiple_of(sub * band, band), band)
    flux[...] = factor[rows, :] * (sst[...] - out[groups - 1, depth - 1])


def ocean_kernel(
    width, n_sub, place, ids, flux, from_east_flux, temp_in, diffusivity, mask_in, inverse, weights,
    from_west, from_east, even_rows, odd_rows, folded, out, window, surface,
):
    sub = place[0]
    band = flux.shape[0]
    levels, rows, cells = temp_in.shape
    for side, source in enumerate((flux, from_east_flux)):
        for g in range(2):
            at = (side * 2 + g) * band
            window[at : at + band, :] = source[:, g * LANES : (g + 1) * LANES]

    @pl.loop(0, rows)
    def _(row):
        surface[pl.ds(row, 1), :] = mat_vec(ids, row * width, width, window, weights)

    temp = temp_in[...]
    mask = mask_in[...].astype(F32)
    even = lax.rem(sub, 2) == 0
    own_south = temp[:, 0, :]
    south_row = jnp.where(even, jnp.where(sub == 0, own_south, odd_rows[...]), even_rows[...])
    north_row = jnp.where(
        even, even_rows[...], jnp.where(sub == n_sub - 1, folded[...], odd_rows[...])
    )
    south = jnp.concatenate([south_row[:, None, :], temp[:, :-1, :]], axis=1)
    north = jnp.concatenate([temp[:, 1:, :], north_row[:, None, :]], axis=1)

    def column(message):
        turned = message[16:24, :].T
        return jnp.concatenate([turned[:, 0:1], turned[:, 1:2]], axis=0)

    flat = temp.reshape(levels * rows, cells)
    lane = lax.broadcasted_iota(jnp.int32, flat.shape, 1)
    west = jnp.where(lane == 0, column(from_west), pltpu.roll(flat, 1, 1))
    east = jnp.where(lane == cells - 1, column(from_east), pltpu.roll(flat, cells - 1, 1))
    lap = (west + east).reshape(temp.shape) + north + south - 4.0 * temp
    stepped = mask[None] * (temp + diffusivity[...][None] * lap)
    heated = stepped[0] + mask * surface[...]
    turned = jnp.swapaxes(stepped, 0, 1)
    level = lax.broadcasted_iota(jnp.int32, (levels, cells), 0)
    high, low = split(inverse[...])
    made = []
    for row in range(rows):
        here = jnp.where(level == 0, heated[row : row + 1, :], turned[row])
        x_high, x_low = split(here)
        made.append(
            jnp.dot(high, x_high, preferred_element_type=F32)
            + jnp.dot(high, x_low, preferred_element_type=F32)
            + jnp.dot(low, x_high, preferred_element_type=F32)
        )
    out[...] = jnp.swapaxes(jnp.stack(made), 0, 1)


def place_kernel(parts, out, sems):
    band = parts.shape[2]
    copies = [
        pltpu.make_async_copy(parts.at[b], out.at[:, pl.ds(b * band, band), :], sems.at[b])
        for b in range(parts.shape[0])
    ]
    for copy in copies:
        copy.start()
    for copy in copies:
        copy.wait()


def pair_exchanges(n_lon, n_sub):
    first, second = [], []
    for lon in range(n_lon):
        at = lon * n_sub
        for south in range(n_sub - 1):
            pairs = first if south % 2 == 0 else second
            pairs += [(at + south, at + south + 1), (at + south + 1, at + south)]
        second.append((at + n_sub - 1, (n_lon - 1 - lon) * n_sub + n_sub - 1))
    return first, second


def per_device(
    atm_tracer,
    courant,
    column_inverse,
    heat_exchange_factor,
    ocean_temp,
    diffusivity,
    ocean_inverse,
    land_mask,
    weights,
    a2o_src,
    a2o_wgt,
    o2a_src,
    o2a_wgt,
):
    lon_index = lax.axis_index("lon")
    sub_index = lax.axis_index("sub")
    n_lon = lax.axis_size("lon")
    n_sub = lax.axis_size("sub")
    lev_dev, alat, alon_dev = atm_tracer.shape
    groups = alon_dev // LANES
    ngroups = groups * n_lon
    olev, olat_dev, olon_dev = ocean_temp.shape
    aband = alat // n_sub
    width = o2a_src.shape[2]
    ocean_flat = ocean_temp.reshape(olev * olat_dev, olon_dev)
    place = jnp.reshape(sub_index, (1,))

    east_msg, west_msg = kernel_call(
        edges_kernel, (shape(32, LANES), shape(24, LANES)), [VMEM] * 3, (VMEM, VMEM),
        flops=2 * MIB, moved=2 * MIB, name="edges",
    )(atm_tracer, ocean_flat, land_mask)
    up = [(i, (i + 1) % n_lon) for i in range(n_lon)]
    down = [(b, a) for a, b in up]
    from_west = lax.ppermute(east_msg, "lon", up)
    from_east = lax.ppermute(west_msg, "lon", down)

    advected = kernel_call(
        advect_kernel, shape(n_sub, aband, lev_dev, alon_dev), [VMEM] * 4, VMEM,
        scratch=[pltpu.VMEM((LANES, 32), F32), pltpu.VMEM((LANES, 24), F32)],
        flops=10 * MIB, moved=6 * MIB, name="advect",
    )(atm_tracer, courant, from_west, from_east)
    columns = lax.all_to_all(advected, "sub", split_axis=0, concat_axis=0, tiled=True)

    even = lax.rem(sub_index, 2) == 0
    top_row, low_row = ocean_temp[:, olat_dev - 1, :], ocean_temp[:, 0, :]
    first, second = pair_exchanges(n_lon, n_sub)
    even_rows = lax.ppermute(jnp.where(even, top_row, low_row), ("lon", "sub"), first)
    odd_rows = lax.ppermute(jnp.where(even, low_row, top_row), ("lon", "sub"), second)
    folded = jnp.flip(odd_rows, axis=1)

    band_src = lax.dynamic_slice_in_dim(o2a_src, sub_index * aband, aband, 0).reshape(-1)
    band_wgt = lax.dynamic_slice_in_dim(o2a_wgt, sub_index * aband, aband, 0).reshape(-1)
    tile = jnp.remainder(band_src % n_lon - lon_index + 1, n_lon)
    sea_ids = tile * olat_dev + band_src // n_lon - sub_index * olat_dev
    sst = kernel_call(
        functools.partial(sst_kernel, width), shape(aband, alon_dev), [SMEM] + [VMEM] * 4, VMEM,
        scratch=[pltpu.VMEM((2 * olat_dev, LANES), F32), pltpu.VMEM((groups, aband, LANES), F32)],
        flops=8 * MIB, moved=8 * MIB, name="sst",
    )(jnp.concatenate([sea_ids, band_wgt]), from_west, ocean_flat, land_mask, weights)

    solved, flux_band = kernel_call(
        solve_kernel, (shape(n_sub, lev_dev, aband, alon_dev), shape(aband, alon_dev)),
        [SMEM] + [VMEM] * 4, (VMEM, VMEM),
        scratch=[pltpu.VMEM((aband, lev_dev * n_sub, alon_dev), F32)],
        flops=400 * MIB, moved=4 * MIB, name="solve",
    )(place, columns, column_inverse, heat_exchange_factor, sst)
    parts = lax.all_to_all(solved, "sub", split_axis=0, concat_axis=0, tiled=True)

    east_flux = lax.ppermute(flux_band, "lon", down)
    src = a2o_src.reshape(-1)
    group = jnp.remainder(src % ngroups - lon_index * groups, ngroups)
    flux_ids = group * aband + src // ngroups - sub_index * aband
    ocean_new = kernel_call(
        functools.partial(ocean_kernel, width, n_sub), shape(olev, olat_dev, olon_dev),
        [SMEM] * 2 + [VMEM] * 12, VMEM,
        scratch=[pltpu.VMEM((4 * aband, LANES), F32), pltpu.VMEM((olat_dev, LANES), F32)],
        flops=8 * MIB, moved=8 * MIB, name="ocean",
    )(
        place, jnp.concatenate([flux_ids, a2o_wgt.reshape(-1)]), flux_band, east_flux, ocean_temp,
        diffusivity, land_mask, ocean_inverse, weights, from_west, from_east, even_rows, odd_rows, folded,
    )

    returned = kernel_call(
        place_kernel, shape(lev_dev, alat, alon_dev), [VMEM], ANY,
        scratch=[pltpu.SemaphoreType.DMA((n_sub,))], moved=4 * MIB, name="place",
    )(parts)
    return returned, ocean_new, flux_band


def solution(mesh):
    return jax.shard_map(
        per_device,
        mesh=mesh,
        in_specs=(
            P("sub", None, "lon"),
            P("sub", None, "lon"),
            P(),
            P(None, "lon"),
            P(None, "sub", "lon"),
            P("sub", "lon"),
            P(),
            P("sub", "lon"),
            P(),
            P("sub", "lon", None),
            P("sub", "lon", None),
            P(None, "lon", None),
            P(None, "lon", None),
        ),
        out_specs=(P("sub", None, "lon"), P(None, "sub", "lon"), P("sub", "lon")),
        check_vma=False,
    )
```

```python
import functools

import jax
import jax.numpy as jnp
from jax import lax
from jax.experimental import pallas as pl
from jax.experimental.pallas import tpu as pltpu
from jax.sharding import PartitionSpec as P

F32 = jnp.float32
BF16 = jnp.bfloat16
VMEM = pl.BlockSpec(memory_space=pltpu.VMEM)
SMEM = pl.BlockSpec(memory_space=pltpu.SMEM)
ANY = pl.BlockSpec(memory_space=pl.ANY)
MIB = 1 << 20
LANES = 128
PIECES = 4
HBM = pl.BlockSpec(memory_space=pltpu.HBM)


def kernel_call(body, out_shape, in_specs, out_specs, scratch=(), flops=0, moved=0, limit=16, name=None):
    return pl.pallas_call(
        body,
        out_shape=out_shape,
        in_specs=in_specs,
        out_specs=out_specs,
        scratch_shapes=list(scratch),
        compiler_params=pltpu.CompilerParams(vmem_limit_bytes=limit * MIB),
        cost_estimate=pl.CostEstimate(flops=flops, bytes_accessed=moved, transcendentals=0),
        name=name,
    )


def shape(*dims):
    return jax.ShapeDtypeStruct(dims, F32)


def in_hbm(*dims):
    return pltpu.HBM(dims, F32)


def in_vmem(*dims):
    return pltpu.VMEM(dims, F32)


def stays(value):
    return pltpu.with_memory_space_constraint(value, pltpu.HBM)


def split(value):
    high = value.astype(BF16)
    return high, (value - high.astype(F32)).astype(BF16)


def edges_kernel(atm_in, ocean_in, mask_in, east_msg, west_msg, atm, ocean, mask, sems):
    levels, rows, cells = atm.shape
    step = levels // PIECES
    pieces = [pl.ds(piece * step, step) for piece in range(PIECES)]
    copies = [pltpu.make_async_copy(atm_in.at[p], atm.at[p], sems.at[i]) for i, p in enumerate(pieces)]
    copies.append(pltpu.make_async_copy(ocean_in, ocean, sems.at[PIECES]))
    copies.append(pltpu.make_async_copy(mask_in, mask, sems.at[PIECES + 1]))
    for copy in copies:
        copy.start()
    lane = lax.broadcasted_iota(jnp.int32, (LANES, LANES), 1)
    last = jnp.zeros((LANES, LANES), F32)
    first = jnp.zeros((LANES, LANES), F32)
    for piece in range(PIECES):
        copies[piece].wait()
        for level in range(piece * step, (piece + 1) * step):
            last = jnp.where(lane == level, atm[level, :, cells - 1 : cells], last)
            first = jnp.where(lane == level, atm[level, :, 0:1], first)
    for copy in copies[PIECES:]:
        copy.wait()
    for part in range(2):
        tile = slice(part * LANES, (part + 1) * LANES)
        last = jnp.where(lane == levels + part, ocean[tile, LANES - 1 : LANES], last)
        first = jnp.where(lane == levels + part, ocean[tile, 0:1], first)
    east_msg[:24, :] = last.T[:24, :]
    east_msg[24:, :] = mask[...].astype(F32) * ocean[:8, :]
    west_msg[...] = first.T[:24, :]


def advect_kernel(atm, courant, from_west, from_east, out, west_cols, east_cols, held, sems):
    levels, _, cells = atm.shape
    band = out.shape[1]
    west_cols[...] = from_west[...].T
    east_cols[...] = from_east[...].T
    lane = lax.broadcasted_iota(jnp.int32, (band, cells), 1)

    @pl.loop(0, out.shape[0])
    def _(dest):
        rows = pl.ds(pl.multiple_of(dest * band, band), band)
        made = []
        for level in range(levels):
            here = atm[level, rows, :]
            speed = courant[level, rows, :]
            west = jnp.where(lane == 0, west_cols[rows, level : level + 1], pltpu.roll(here, 1, 1))
            east = jnp.where(
                lane == cells - 1, east_cols[rows, level : level + 1], pltpu.roll(here, cells - 1, 1)
            )
            made.append(
                here
                - jnp.maximum(speed, 0.0) * (here - west)
                - jnp.minimum(speed, 0.0) * (east - here)
            )
        held[dest] = jnp.swapaxes(jnp.stack(made), 0, 1)
        pltpu.make_async_copy(held.at[dest], out.at[dest], sems.at[dest]).start()

    for dest in range(out.shape[0]):
        pltpu.make_async_copy(held.at[dest], out.at[dest], sems.at[dest]).wait()


def mat_vec(ids, first, count, source, weights):
    total = jnp.zeros(weights.shape[1:], F32)
    half = ids.shape[0] // 2
    for k in range(count):
        block = source[pl.ds(ids[first + k], 1), :]
        total = total + weights[ids[half + first + k]] * block
    return jnp.sum(total.T, axis=0, keepdims=True)


def sst_kernel(width, place, ids, from_west, ocean, mask, weights, sst, even_msg, odd_msg, window, halves):
    tile_rows = mask.shape[0]
    tile = ocean[...].reshape(-1, tile_rows, LANES)
    even = lax.rem(place[0], 2) == 0
    low, top = tile[:, 0, :], tile[:, tile_rows - 1, :]
    even_msg[...] = jnp.where(even, top, low)
    odd_msg[...] = jnp.where(even, low, top)
    window[:8, :] = from_west[24:32, :]
    window[8:, :] = mask[...].astype(F32) * ocean[:8, :]
    rows = sst.shape[0]

    @pl.loop(0, rows)
    def _(row):
        for g in range(2):
            halves[g, pl.ds(row, 1), :] = mat_vec(ids, (row * 2 + g) * width, width, window, weights)

    for g in range(2):
        sst[:, g * LANES : (g + 1) * LANES] = halves[g]


def solve_kernel(place, columns, inverse, factor, sst, even_rows, odd_rows, out, flux, held, turned, sems):
    sub = place[0]
    groups, band, depth, cells = columns.shape
    levels = groups * depth
    high, low = split(inverse[sub])
    twice = jnp.concatenate([high, high], axis=1)

    def solve_row(row, _):
        here = columns[:, row].reshape(levels, cells)
        x_high, x_low = split(here)
        held[row] = jnp.dot(
            twice, jnp.concatenate([x_high, x_low], axis=0), preferred_element_type=F32
        ) + jnp.dot(low, x_high, preferred_element_type=F32)
        return 0

    lax.fori_loop(0, band, solve_row, 0, unroll=4)
    copies = []
    for group in range(groups):
        turned[group] = jnp.swapaxes(held[:, group * depth : (group + 1) * depth, :], 0, 1)
        copies.append(pltpu.make_async_copy(turned.at[group], out.at[group], sems.at[group]))
        copies[-1].start()
    rows = pl.ds(pl.multiple_of(sub * band, band), band)
    flux[...] = factor[rows, :] * (sst[...] - turned[groups - 1, depth - 1])
    for copy in copies:
        copy.wait()


def ocean_kernel(
    n_sub, place, temp_in, diffusivity, mask_in, inverse,
    from_west, from_east, even_rows, odd_rows, folded, out,
):
    sub = place[0]
    levels, rows, cells = temp_in.shape
    temp = temp_in[...]
    mask = mask_in[...].astype(F32)
    even = lax.rem(sub, 2) == 0
    own_south = temp[:, 0, :]
    south_row = jnp.where(even, jnp.where(sub == 0, own_south, odd_rows[...]), even_rows[...])
    north_row = jnp.where(
        even, even_rows[...], jnp.where(sub == n_sub - 1, folded[...], odd_rows[...])
    )
    south = jnp.concatenate([south_row[:, None, :], temp[:, :-1, :]], axis=1)
    north = jnp.concatenate([temp[:, 1:, :], north_row[:, None, :]], axis=1)

    def column(message):
        side = message[16:24, :].T
        return jnp.concatenate([side[:, 0:1], side[:, 1:2]], axis=0)

    flat = temp.reshape(levels * rows, cells)
    lane = lax.broadcasted_iota(jnp.int32, flat.shape, 1)
    west = jnp.where(lane == 0, column(from_west), pltpu.roll(flat, 1, 1))
    east = jnp.where(lane == cells - 1, column(from_east), pltpu.roll(flat, cells - 1, 1))
    lap = (west + east).reshape(temp.shape) + north + south - 4.0 * temp
    stepped = mask[None] * (temp + diffusivity[...][None] * lap)
    by_row = jnp.swapaxes(stepped, 0, 1)
    high, low = split(inverse[...])
    made = []
    for row in range(rows):
        x_high, x_low = split(by_row[row])
        made.append(
            jnp.dot(high, x_high, preferred_element_type=F32)
            + jnp.dot(high, x_low, preferred_element_type=F32)
            + jnp.dot(low, x_high, preferred_element_type=F32)
        )
    out[...] = jnp.swapaxes(jnp.stack(made), 0, 1)


def last_kernel(
    width, ids, flux, from_east_flux, weights, mask, inverse, before, parts, out, ocean,
    window, picked, pick_sems, sems,
):
    entries = picked.shape[0]
    picks = [
        pltpu.make_async_copy(weights.at[ids[entries + i]], picked.at[i], pick_sems.at[i])
        for i in range(entries)
    ]
    for pick in picks:
        pick.start()
    band = parts.shape[2]
    copies = [
        pltpu.make_async_copy(parts.at[b], out.at[:, pl.ds(b * band, band), :], sems.at[b])
        for b in range(parts.shape[0])
    ]
    for copy in copies:
        copy.start()
    for side, source in enumerate((flux, from_east_flux)):
        for g in range(2):
            at = (side * 2 + g) * band
            window[at : at + band, :] = source[:, g * LANES : (g + 1) * LANES]
    levels, rows, _ = before.shape
    made = []
    for row in range(rows):
        total = jnp.zeros((LANES, LANES), F32)
        for k in range(row * width, (row + 1) * width):
            picks[k].wait()
            total = total + picked[k] * window[pl.ds(ids[k], 1), :]
        made.append(jnp.sum(total.T, axis=0, keepdims=True))
    heat = mask[...].astype(F32) * jnp.concatenate(made, axis=0)
    for level in range(levels):
        ocean[level] = before[level] + inverse[level : level + 1, 0:1] * heat
    for copy in copies:
        copy.wait()


def pair_exchanges(n_lon, n_sub):
    first, second = [], []
    for lon in range(n_lon):
        at = lon * n_sub
        for south in range(n_sub - 1):
            pairs = first if south % 2 == 0 else second
            pairs += [(at + south, at + south + 1), (at + south + 1, at + south)]
        second.append((at + n_sub - 1, (n_lon - 1 - lon) * n_sub + n_sub - 1))
    return first, second


def per_device(
    atm_tracer,
    courant,
    column_inverse,
    heat_exchange_factor,
    ocean_temp,
    diffusivity,
    ocean_inverse,
    land_mask,
    weights,
    a2o_src,
    a2o_wgt,
    o2a_src,
    o2a_wgt,
):
    lon_index = lax.axis_index("lon")
    sub_index = lax.axis_index("sub")
    n_lon = lax.axis_size("lon")
    n_sub = lax.axis_size("sub")
    lev_dev, alat, alon_dev = atm_tracer.shape
    groups = alon_dev // LANES
    ngroups = groups * n_lon
    olev, olat_dev, olon_dev = ocean_temp.shape
    aband = alat // n_sub
    width = o2a_src.shape[2]
    ocean_flat = ocean_temp.reshape(olev * olat_dev, olon_dev)
    place = jnp.reshape(sub_index, (1,))

    east_msg, west_msg, atm_here = kernel_call(
        edges_kernel, (shape(32, LANES), shape(24, LANES), in_vmem(lev_dev, alat, alon_dev)), [HBM] * 3, (VMEM,) * 3,
        scratch=[
            pltpu.VMEM(ocean_flat.shape, F32), pltpu.VMEM(land_mask.shape, land_mask.dtype),
            pltpu.SemaphoreType.DMA((PIECES + 2,)),
        ],
        flops=2 * MIB, moved=2 * MIB, name="edges",
    )(stays(atm_tracer), stays(ocean_flat), stays(land_mask))
    up = [(i, (i + 1) % n_lon) for i in range(n_lon)]
    down = [(b, a) for a, b in up]
    from_west = lax.ppermute(east_msg, "lon", up)
    from_east = lax.ppermute(west_msg, "lon", down)

    advected = kernel_call(
        advect_kernel, in_hbm(n_sub, aband, lev_dev, alon_dev), [VMEM] * 4, HBM,
        scratch=[
            pltpu.VMEM((LANES, 32), F32), pltpu.VMEM((LANES, 24), F32),
            pltpu.VMEM((n_sub, aband, lev_dev, alon_dev), F32), pltpu.SemaphoreType.DMA((n_sub,)),
        ],
        flops=10 * MIB, moved=6 * MIB, name="advect",
    )(atm_here, courant, from_west, from_east)
    columns = lax.all_to_all(advected, "sub", split_axis=0, concat_axis=0, tiled=True)

    band_src = lax.dynamic_slice_in_dim(o2a_src, sub_index * aband, aband, 0).reshape(-1)
    band_wgt = lax.dynamic_slice_in_dim(o2a_wgt, sub_index * aband, aband, 0).reshape(-1)
    tile = jnp.remainder(band_src % n_lon - lon_index + 1, n_lon)
    sea_ids = tile * olat_dev + band_src // n_lon - sub_index * olat_dev
    sst, even_msg, odd_msg = kernel_call(
        functools.partial(sst_kernel, width),
        (shape(aband, alon_dev), shape(olev, LANES), shape(olev, LANES)), [SMEM] * 2 + [VMEM] * 4, (VMEM,) * 3,
        scratch=[pltpu.VMEM((2 * olat_dev, LANES), F32), pltpu.VMEM((groups, aband, LANES), F32)],
        flops=8 * MIB, moved=8 * MIB, name="sst",
    )(place, jnp.concatenate([sea_ids, band_wgt]), from_west, ocean_flat, land_mask, weights)
    first, second = pair_exchanges(n_lon, n_sub)
    even_rows = lax.ppermute(even_msg, ("lon", "sub"), first)
    odd_rows = lax.ppermute(odd_msg, ("lon", "sub"), second)
    folded = jnp.flip(odd_rows, axis=1)

    solved, flux_band = kernel_call(
        solve_kernel, (in_hbm(n_sub, lev_dev, aband, alon_dev), shape(aband, alon_dev)),
        [SMEM] + [VMEM] * 4 + [ANY] * 2, (HBM, VMEM),
        scratch=[
            pltpu.VMEM((aband, lev_dev * n_sub, alon_dev), F32),
            pltpu.VMEM((n_sub, lev_dev, aband, alon_dev), F32), pltpu.SemaphoreType.DMA((n_sub,)),
        ],
        flops=400 * MIB, moved=4 * MIB, name="solve",
    )(place, columns, column_inverse, heat_exchange_factor, sst, even_rows, odd_rows)
    parts = lax.all_to_all(solved, "sub", split_axis=0, concat_axis=0, tiled=True)
    east_flux = lax.ppermute(flux_band, "lon", down)

    src = a2o_src.reshape(-1)
    group = jnp.remainder(src % ngroups - lon_index * groups, ngroups)
    flux_ids = group * aband + src // ngroups - sub_index * aband
    entries = src.shape[0]
    before = kernel_call(
        functools.partial(ocean_kernel, n_sub), shape(olev, olat_dev, olon_dev),
        [SMEM] + [VMEM] * 9, VMEM, flops=8 * MIB, moved=MIB, name="ocean",
    )(
        place, ocean_temp, diffusivity, land_mask, ocean_inverse,
        from_west, from_east, even_rows, odd_rows, folded,
    )
    returned, ocean_new = kernel_call(
        functools.partial(last_kernel, width), (shape(lev_dev, alat, alon_dev), shape(olev, olat_dev, olon_dev)),
        [SMEM] + [VMEM] * 2 + [HBM] + [VMEM] * 4, (HBM, VMEM),
        scratch=[
            pltpu.VMEM((4 * aband, LANES), F32), pltpu.VMEM((entries, LANES, LANES), F32),
            pltpu.SemaphoreType.DMA((entries,)), pltpu.SemaphoreType.DMA((n_sub,)),
        ],
        moved=6 * MIB, name="last",
    )(
        jnp.concatenate([flux_ids, a2o_wgt.reshape(-1)]), flux_band, east_flux, stays(weights),
        land_mask, ocean_inverse, before, parts,
    )
    return returned, ocean_new, flux_band


def solution(mesh):
    return jax.shard_map(
        per_device,
        mesh=mesh,
        in_specs=(
            P("sub", None, "lon"),
            P("sub", None, "lon"),
            P(),
            P(None, "lon"),
            P(None, "sub", "lon"),
            P("sub", "lon"),
            P(),
            P("sub", "lon"),
            P(),
            P("sub", "lon", None),
            P("sub", "lon", None),
            P(None, "lon", None),
            P(None, "lon", None),
        ),
        out_specs=(P("sub", None, "lon"), P(None, "sub", "lon"), P("sub", "lon")),
        check_vma=False,
    )
```

```python
import functools

import jax
import jax.numpy as jnp
from jax import lax
from jax.experimental import pallas as pl
from jax.experimental.pallas import tpu as pltpu
from jax.sharding import PartitionSpec as P

F32 = jnp.float32
BF16 = jnp.bfloat16
VMEM = pl.BlockSpec(memory_space=pltpu.VMEM)
SMEM = pl.BlockSpec(memory_space=pltpu.SMEM)
ANY = pl.BlockSpec(memory_space=pl.ANY)
MIB = 1 << 20
LANES = 128
PIECES = 4
HBM = pl.BlockSpec(memory_space=pltpu.HBM)


def kernel_call(body, out_shape, in_specs, out_specs, scratch=(), flops=0, moved=0, limit=16, name=None):
    return pl.pallas_call(
        body,
        out_shape=out_shape,
        in_specs=in_specs,
        out_specs=out_specs,
        scratch_shapes=list(scratch),
        compiler_params=pltpu.CompilerParams(vmem_limit_bytes=limit * MIB),
        cost_estimate=pl.CostEstimate(flops=flops, bytes_accessed=moved, transcendentals=0),
        name=name,
    )


def shape(*dims):
    return jax.ShapeDtypeStruct(dims, F32)


def in_hbm(*dims):
    return pltpu.HBM(dims, F32)


def in_vmem(*dims):
    return pltpu.VMEM(dims, F32)


def stays(value):
    return pltpu.with_memory_space_constraint(value, pltpu.HBM)


def split(value):
    high = value.astype(BF16)
    return high, (value - high.astype(F32)).astype(BF16)


def edges_kernel(atm_in, ocean_in, mask_in, east_msg, west_msg, atm, ocean, mask, sems):
    levels, rows, cells = atm.shape
    step = levels // PIECES
    pieces = [pl.ds(piece * step, step) for piece in range(PIECES)]
    copies = [pltpu.make_async_copy(atm_in.at[p], atm.at[p], sems.at[i]) for i, p in enumerate(pieces)]
    copies.append(pltpu.make_async_copy(ocean_in, ocean, sems.at[PIECES]))
    copies.append(pltpu.make_async_copy(mask_in, mask, sems.at[PIECES + 1]))
    for copy in copies:
        copy.start()
    lane = lax.broadcasted_iota(jnp.int32, (LANES, LANES), 1)
    last = jnp.zeros((LANES, LANES), F32)
    first = jnp.zeros((LANES, LANES), F32)
    for piece in range(PIECES):
        copies[piece].wait()
        for level in range(piece * step, (piece + 1) * step):
            last = jnp.where(lane == level, atm[level, :, cells - 1 : cells], last)
            first = jnp.where(lane == level, atm[level, :, 0:1], first)
    for copy in copies[PIECES:]:
        copy.wait()
    for part in range(2):
        tile = slice(part * LANES, (part + 1) * LANES)
        last = jnp.where(lane == levels + part, ocean[tile, LANES - 1 : LANES], last)
        first = jnp.where(lane == levels + part, ocean[tile, 0:1], first)
    east_msg[:24, :] = last.T[:24, :]
    east_msg[24:, :] = mask[...].astype(F32) * ocean[:8, :]
    west_msg[...] = first.T[:24, :]


def advect_kernel(atm, courant, from_west, from_east, out, west_cols, east_cols, held, sems):
    levels, _, cells = atm.shape
    band = out.shape[1]
    west_cols[...] = from_west[...].T
    east_cols[...] = from_east[...].T
    lane = lax.broadcasted_iota(jnp.int32, (band, cells), 1)

    @pl.loop(0, out.shape[0])
    def _(dest):
        rows = pl.ds(pl.multiple_of(dest * band, band), band)
        made = []
        for level in range(levels):
            here = atm[level, rows, :]
            speed = courant[level, rows, :]
            west = jnp.where(lane == 0, west_cols[rows, level : level + 1], pltpu.roll(here, 1, 1))
            east = jnp.where(
                lane == cells - 1, east_cols[rows, level : level + 1], pltpu.roll(here, cells - 1, 1)
            )
            made.append(
                here
                - jnp.maximum(speed, 0.0) * (here - west)
                - jnp.minimum(speed, 0.0) * (east - here)
            )
        held[dest] = jnp.swapaxes(jnp.stack(made), 0, 1)
        pltpu.make_async_copy(held.at[dest], out.at[dest], sems.at[dest]).start()

    for dest in range(out.shape[0]):
        pltpu.make_async_copy(held.at[dest], out.at[dest], sems.at[dest]).wait()


def mat_vec(ids, first, count, source, weights):
    total = jnp.zeros(weights.shape[1:], F32)
    half = ids.shape[0] // 2
    for k in range(count):
        block = source[pl.ds(ids[first + k], 1), :]
        total = total + weights[ids[half + first + k]] * block
    return jnp.sum(total.T, axis=0, keepdims=True)


def sst_kernel(width, place, ids, from_west, ocean, mask, weights, sst, even_msg, odd_msg, window, halves):
    tile_rows = mask.shape[0]
    tile = ocean[...].reshape(-1, tile_rows, LANES)
    even = lax.rem(place[0], 2) == 0
    low, top = tile[:, 0, :], tile[:, tile_rows - 1, :]
    even_msg[...] = jnp.where(even, top, low)
    odd_msg[...] = jnp.where(even, low, top)
    window[:8, :] = from_west[24:32, :]
    window[8:, :] = mask[...].astype(F32) * ocean[:8, :]
    rows = sst.shape[0]

    @pl.loop(0, rows)
    def _(row):
        for g in range(2):
            halves[g, pl.ds(row, 1), :] = mat_vec(ids, (row * 2 + g) * width, width, window, weights)

    for g in range(2):
        sst[:, g * LANES : (g + 1) * LANES] = halves[g]


def solve_kernel(place, columns, inverse, factor, sst, even_rows, odd_rows, out, flux, held, turned, sems):
    sub = place[0]
    groups, band, depth, cells = columns.shape
    levels = groups * depth
    high, low = split(inverse[sub])
    twice = jnp.concatenate([high, high], axis=1)

    def solve_row(row, _):
        here = columns[:, row].reshape(levels, cells)
        x_high, x_low = split(here)
        held[row] = jnp.dot(
            twice, jnp.concatenate([x_high, x_low], axis=0), preferred_element_type=F32
        ) + jnp.dot(low, x_high, preferred_element_type=F32)
        return 0

    lax.fori_loop(0, band, solve_row, 0, unroll=4)
    copies = []
    for group in range(groups):
        turned[group] = jnp.swapaxes(held[:, group * depth : (group + 1) * depth, :], 0, 1)
        copies.append(pltpu.make_async_copy(turned.at[group], out.at[group], sems.at[group]))
        copies[-1].start()
    rows = pl.ds(pl.multiple_of(sub * band, band), band)
    flux[...] = factor[rows, :] * (sst[...] - turned[groups - 1, depth - 1])
    for copy in copies:
        copy.wait()


def ocean_kernel(
    width, n_sub, place, ids, flux, from_east_flux, weights, temp_in, diffusivity, mask_in, inverse,
    from_west, from_east, even_rows, odd_rows, folded, out, window, picked, sems,
):
    sub = place[0]
    band = flux.shape[0]
    entries = picked.shape[0]
    picks = [
        pltpu.make_async_copy(weights.at[ids[entries + i]], picked.at[i], sems.at[i])
        for i in range(entries)
    ]
    for pick in picks:
        pick.start()
    for side, source in enumerate((flux, from_east_flux)):
        for g in range(2):
            at = (side * 2 + g) * band
            window[at : at + band, :] = source[:, g * LANES : (g + 1) * LANES]
    levels, rows, cells = temp_in.shape
    temp = temp_in[...]
    mask = mask_in[...].astype(F32)
    even = lax.rem(sub, 2) == 0
    own_south = temp[:, 0, :]
    south_row = jnp.where(even, jnp.where(sub == 0, own_south, odd_rows[...]), even_rows[...])
    north_row = jnp.where(
        even, even_rows[...], jnp.where(sub == n_sub - 1, folded[...], odd_rows[...])
    )
    south = jnp.concatenate([south_row[:, None, :], temp[:, :-1, :]], axis=1)
    north = jnp.concatenate([temp[:, 1:, :], north_row[:, None, :]], axis=1)

    def column(message):
        side = message[16:24, :].T
        return jnp.concatenate([side[:, 0:1], side[:, 1:2]], axis=0)

    flat = temp.reshape(levels * rows, cells)
    lane = lax.broadcasted_iota(jnp.int32, flat.shape, 1)
    west = jnp.where(lane == 0, column(from_west), pltpu.roll(flat, 1, 1))
    east = jnp.where(lane == cells - 1, column(from_east), pltpu.roll(flat, cells - 1, 1))
    lap = (west + east).reshape(temp.shape) + north + south - 4.0 * temp
    stepped = mask[None] * (temp + diffusivity[...][None] * lap)
    by_row = jnp.swapaxes(stepped, 0, 1)
    level = lax.broadcasted_iota(jnp.int32, (levels, cells), 0)
    high, low = split(inverse[...])
    made = []
    for row in range(rows):
        total = jnp.zeros((LANES, LANES), F32)
        for k in range(row * width, (row + 1) * width):
            picks[k].wait()
            total = total + picked[k] * window[pl.ds(ids[k], 1), :]
        heat = mask[row : row + 1, :] * jnp.sum(total.T, axis=0, keepdims=True)
        x_high, x_low = split(by_row[row] + jnp.where(level == 0, heat, 0.0))
        made.append(
            jnp.dot(high, x_high, preferred_element_type=F32)
            + jnp.dot(high, x_low, preferred_element_type=F32)
            + jnp.dot(low, x_high, preferred_element_type=F32)
        )
    out[...] = jnp.swapaxes(jnp.stack(made), 0, 1)


def place_kernel(parts, out, sems):
    band = parts.shape[2]
    copies = [
        pltpu.make_async_copy(parts.at[b], out.at[:, pl.ds(b * band, band), :], sems.at[b])
        for b in range(parts.shape[0])
    ]
    for copy in copies:
        copy.start()
    for copy in copies:
        copy.wait()


def pair_exchanges(n_lon, n_sub):
    first, second = [], []
    for lon in range(n_lon):
        at = lon * n_sub
        for south in range(n_sub - 1):
            pairs = first if south % 2 == 0 else second
            pairs += [(at + south, at + south + 1), (at + south + 1, at + south)]
        second.append((at + n_sub - 1, (n_lon - 1 - lon) * n_sub + n_sub - 1))
    return first, second


def per_device(
    atm_tracer,
    courant,
    column_inverse,
    heat_exchange_factor,
    ocean_temp,
    diffusivity,
    ocean_inverse,
    land_mask,
    weights,
    a2o_src,
    a2o_wgt,
    o2a_src,
    o2a_wgt,
):
    lon_index = lax.axis_index("lon")
    sub_index = lax.axis_index("sub")
    n_lon = lax.axis_size("lon")
    n_sub = lax.axis_size("sub")
    lev_dev, alat, alon_dev = atm_tracer.shape
    groups = alon_dev // LANES
    ngroups = groups * n_lon
    olev, olat_dev, olon_dev = ocean_temp.shape
    aband = alat // n_sub
    width = o2a_src.shape[2]
    ocean_flat = ocean_temp.reshape(olev * olat_dev, olon_dev)
    place = jnp.reshape(sub_index, (1,))

    east_msg, west_msg, atm_here = kernel_call(
        edges_kernel, (shape(32, LANES), shape(24, LANES), in_vmem(lev_dev, alat, alon_dev)), [HBM] * 3, (VMEM,) * 3,
        scratch=[
            pltpu.VMEM(ocean_flat.shape, F32), pltpu.VMEM(land_mask.shape, land_mask.dtype),
            pltpu.SemaphoreType.DMA((PIECES + 2,)),
        ],
        flops=2 * MIB, moved=2 * MIB, name="edges",
    )(stays(atm_tracer), stays(ocean_flat), stays(land_mask))
    up = [(i, (i + 1) % n_lon) for i in range(n_lon)]
    down = [(b, a) for a, b in up]
    from_west = lax.ppermute(east_msg, "lon", up)
    from_east = lax.ppermute(west_msg, "lon", down)

    advected = kernel_call(
        advect_kernel, in_hbm(n_sub, aband, lev_dev, alon_dev), [VMEM] * 4, HBM,
        scratch=[
            pltpu.VMEM((LANES, 32), F32), pltpu.VMEM((LANES, 24), F32),
            pltpu.VMEM((n_sub, aband, lev_dev, alon_dev), F32), pltpu.SemaphoreType.DMA((n_sub,)),
        ],
        flops=10 * MIB, moved=6 * MIB, name="advect",
    )(atm_here, courant, from_west, from_east)
    columns = lax.all_to_all(advected, "sub", split_axis=0, concat_axis=0, tiled=True)

    band_src = lax.dynamic_slice_in_dim(o2a_src, sub_index * aband, aband, 0).reshape(-1)
    band_wgt = lax.dynamic_slice_in_dim(o2a_wgt, sub_index * aband, aband, 0).reshape(-1)
    tile = jnp.remainder(band_src % n_lon - lon_index + 1, n_lon)
    sea_ids = tile * olat_dev + band_src // n_lon - sub_index * olat_dev
    sst, even_msg, odd_msg = kernel_call(
        functools.partial(sst_kernel, width),
        (shape(aband, alon_dev), shape(olev, LANES), shape(olev, LANES)), [SMEM] * 2 + [VMEM] * 4, (VMEM,) * 3,
        scratch=[pltpu.VMEM((2 * olat_dev, LANES), F32), pltpu.VMEM((groups, aband, LANES), F32)],
        flops=8 * MIB, moved=8 * MIB, name="sst",
    )(place, jnp.concatenate([sea_ids, band_wgt]), from_west, ocean_flat, land_mask, weights)
    first, second = pair_exchanges(n_lon, n_sub)
    even_rows = lax.ppermute(even_msg, ("lon", "sub"), first)
    odd_rows = lax.ppermute(odd_msg, ("lon", "sub"), second)
    folded = jnp.flip(odd_rows, axis=1)

    solved, flux_band = kernel_call(
        solve_kernel, (in_hbm(n_sub, lev_dev, aband, alon_dev), shape(aband, alon_dev)),
        [SMEM] + [VMEM] * 4 + [ANY] * 2, (HBM, VMEM),
        scratch=[
            pltpu.VMEM((aband, lev_dev * n_sub, alon_dev), F32),
            pltpu.VMEM((n_sub, lev_dev, aband, alon_dev), F32), pltpu.SemaphoreType.DMA((n_sub,)),
        ],
        flops=400 * MIB, moved=4 * MIB, name="solve",
    )(place, columns, column_inverse, heat_exchange_factor, sst, even_rows, odd_rows)
    parts = lax.all_to_all(solved, "sub", split_axis=0, concat_axis=0, tiled=True)
    east_flux = lax.ppermute(flux_band, "lon", down)

    src = a2o_src.reshape(-1)
    group = jnp.remainder(src % ngroups - lon_index * groups, ngroups)
    flux_ids = group * aband + src // ngroups - sub_index * aband
    entries = src.shape[0]
    ocean_new = kernel_call(
        functools.partial(ocean_kernel, width, n_sub), shape(olev, olat_dev, olon_dev),
        [SMEM] * 2 + [VMEM] * 2 + [HBM] + [VMEM] * 9, VMEM,
        scratch=[
            pltpu.VMEM((4 * aband, LANES), F32), pltpu.VMEM((entries, LANES, LANES), F32),
            pltpu.SemaphoreType.DMA((entries,)),
        ],
        flops=8 * MIB, moved=4 * MIB, name="ocean",
    )(
        place, jnp.concatenate([flux_ids, a2o_wgt.reshape(-1)]), flux_band, east_flux, stays(weights),
        ocean_temp, diffusivity, land_mask, ocean_inverse, from_west, from_east, even_rows, odd_rows, folded,
    )
    returned = kernel_call(
        place_kernel, shape(lev_dev, alat, alon_dev), [VMEM], HBM,
        scratch=[pltpu.SemaphoreType.DMA((n_sub,))], moved=4 * MIB, name="place",
    )(parts)
    return returned, ocean_new, flux_band


def solution(mesh):
    return jax.shard_map(
        per_device,
        mesh=mesh,
        in_specs=(
            P("sub", None, "lon"),
            P("sub", None, "lon"),
            P(),
            P(None, "lon"),
            P(None, "sub", "lon"),
            P("sub", "lon"),
            P(),
            P("sub", "lon"),
            P(),
            P("sub", "lon", None),
            P("sub", "lon", None),
            P(None, "lon", None),
            P(None, "lon", None),
        ),
        out_specs=(P("sub", None, "lon"), P(None, "sub", "lon"), P("sub", "lon")),
        check_vma=False,
    )
```

```python
import functools

import jax
import jax.numpy as jnp
from jax import lax
from jax.experimental import pallas as pl
from jax.experimental.pallas import tpu as pltpu
from jax.sharding import PartitionSpec as P

F32 = jnp.float32
BF16 = jnp.bfloat16
VMEM = pl.BlockSpec(memory_space=pltpu.VMEM)
SMEM = pl.BlockSpec(memory_space=pltpu.SMEM)
ANY = pl.BlockSpec(memory_space=pl.ANY)
MIB = 1 << 20
LANES = 128
PIECES = 8
HBM = pl.BlockSpec(memory_space=pltpu.HBM)


def kernel_call(body, out_shape, in_specs, out_specs, scratch=(), flops=0, moved=0, limit=16, name=None):
    return pl.pallas_call(
        body,
        out_shape=out_shape,
        in_specs=in_specs,
        out_specs=out_specs,
        scratch_shapes=list(scratch),
        compiler_params=pltpu.CompilerParams(vmem_limit_bytes=limit * MIB),
        cost_estimate=pl.CostEstimate(flops=flops, bytes_accessed=moved, transcendentals=0),
        name=name,
    )


def shape(*dims):
    return jax.ShapeDtypeStruct(dims, F32)


def in_hbm(*dims):
    return pltpu.HBM(dims, F32)


def in_vmem(*dims):
    return pltpu.VMEM(dims, F32)


def stays(value):
    return pltpu.with_memory_space_constraint(value, pltpu.HBM)


def split(value):
    high = value.astype(BF16)
    return high, (value - high.astype(F32)).astype(BF16)


def edges_kernel(atm_in, ocean_in, mask_in, east_msg, west_msg, atm, ocean, mask, sems):
    levels, rows, cells = atm.shape
    step = levels // PIECES
    pieces = [pl.ds(piece * step, step) for piece in range(PIECES)]
    copies = [pltpu.make_async_copy(atm_in.at[p], atm.at[p], sems.at[i]) for i, p in enumerate(pieces)]
    copies.append(pltpu.make_async_copy(ocean_in, ocean, sems.at[PIECES]))
    copies.append(pltpu.make_async_copy(mask_in, mask, sems.at[PIECES + 1]))
    for copy in copies:
        copy.start()
    lane = lax.broadcasted_iota(jnp.int32, (LANES, LANES), 1)
    last = jnp.zeros((LANES, LANES), F32)
    first = jnp.zeros((LANES, LANES), F32)
    for piece in range(PIECES):
        copies[piece].wait()
        for level in range(piece * step, (piece + 1) * step):
            last = jnp.where(lane == level, atm[level, :, cells - 1 : cells], last)
            first = jnp.where(lane == level, atm[level, :, 0:1], first)
    for copy in copies[PIECES:]:
        copy.wait()
    for part in range(2):
        tile = slice(part * LANES, (part + 1) * LANES)
        last = jnp.where(lane == levels + part, ocean[tile, LANES - 1 : LANES], last)
        first = jnp.where(lane == levels + part, ocean[tile, 0:1], first)
    east_msg[:24, :] = last.T[:24, :]
    east_msg[24:, :] = mask[...].astype(F32) * ocean[:8, :]
    west_msg[...] = first.T[:24, :]


def base_kernel(atm, courant, out, west_speed, east_speed):
    levels, _, cells = atm.shape
    band = out.shape[1]
    lane = lax.broadcasted_iota(jnp.int32, (band, cells), 1)

    @pl.loop(0, out.shape[0])
    def _(dest):
        rows = pl.ds(pl.multiple_of(dest * band, band), band)
        made = []
        for level in range(levels):
            here = atm[level, rows, :]
            speed = courant[level, rows, :]
            west = jnp.where(lane == 0, 0.0, pltpu.roll(here, 1, 1))
            east = jnp.where(lane == cells - 1, 0.0, pltpu.roll(here, cells - 1, 1))
            made.append(
                here
                - jnp.maximum(speed, 0.0) * (here - west)
                - jnp.minimum(speed, 0.0) * (east - here)
            )
        out[dest] = jnp.swapaxes(jnp.stack(made), 0, 1)

    at = lax.broadcasted_iota(jnp.int32, (LANES, LANES), 1)
    first = jnp.zeros((LANES, LANES), F32)
    last = jnp.zeros((LANES, LANES), F32)
    for level in range(levels):
        first = jnp.where(at == level, courant[level, :, 0:1], first)
        last = jnp.where(at == level, courant[level, :, cells - 1 : cells], last)
    west_speed[...] = jnp.maximum(first.T[:levels, :], 0.0)
    east_speed[...] = jnp.minimum(last.T[:levels, :], 0.0)


def inflow_kernel(base, west_speed, east_speed, from_west, from_east, out, held, sems):
    dests, band, levels, cells = base.shape
    west = west_speed[...] * from_west[:levels, :]
    east = -east_speed[...] * from_east[:levels, :]
    lane = lax.broadcasted_iota(jnp.int32, (levels, LANES), 1)
    copies = []
    for dest in range(dests):
        for row in range(band):
            at = dest * band + row
            held[dest, row, :, :LANES] = base[dest, row, :, :LANES] + jnp.where(
                lane == 0, west[:, at : at + 1], 0.0
            )
            held[dest, row, :, cells - LANES :] = base[dest, row, :, cells - LANES :] + jnp.where(
                lane == LANES - 1, east[:, at : at + 1], 0.0
            )
        copies.append(pltpu.make_async_copy(held.at[dest], out.at[dest], sems.at[dest]))
        copies[-1].start()
    for copy in copies:
        copy.wait()


def mat_vec(ids, first, count, source, weights):
    total = jnp.zeros(weights.shape[1:], F32)
    half = ids.shape[0] // 2
    for k in range(count):
        block = source[pl.ds(ids[first + k], 1), :]
        total = total + weights[ids[half + first + k]] * block
    return jnp.sum(total.T, axis=0, keepdims=True)


def sst_kernel(width, place, ids, from_west, ocean, mask, weights, sst, even_msg, odd_msg, window, halves):
    tile_rows = mask.shape[0]
    tile = ocean[...].reshape(-1, tile_rows, LANES)
    even = lax.rem(place[0], 2) == 0
    low, top = tile[:, 0, :], tile[:, tile_rows - 1, :]
    even_msg[...] = jnp.where(even, top, low)
    odd_msg[...] = jnp.where(even, low, top)
    window[:8, :] = from_west[24:32, :]
    window[8:, :] = mask[...].astype(F32) * ocean[:8, :]
    rows = sst.shape[0]

    @pl.loop(0, rows)
    def _(row):
        for g in range(2):
            halves[g, pl.ds(row, 1), :] = mat_vec(ids, (row * 2 + g) * width, width, window, weights)

    for g in range(2):
        sst[:, g * LANES : (g + 1) * LANES] = halves[g]


def solve_kernel(place, columns, inverse, factor, sst, even_rows, odd_rows, out, flux, held, turned, sems):
    sub = place[0]
    groups, band, depth, cells = columns.shape
    levels = groups * depth
    parts, step = out.shape[1], out.shape[3]
    high, low = split(inverse[sub])
    twice = jnp.concatenate([high, high], axis=1)
    copies = []
    for part in range(parts):
        for row in range(part * step, (part + 1) * step):
            x_high, x_low = split(columns[:, row].reshape(levels, cells))
            held[row] = jnp.dot(
                twice, jnp.concatenate([x_high, x_low], axis=0), preferred_element_type=F32
            ) + jnp.dot(low, x_high, preferred_element_type=F32)
        for group in range(groups):
            turned[group, part] = jnp.swapaxes(
                held[part * step : (part + 1) * step, group * depth : (group + 1) * depth, :], 0, 1
            )
            copies.append(
                pltpu.make_async_copy(
                    turned.at[group, part], out.at[group, part], sems.at[group * parts + part]
                )
            )
            copies[-1].start()
    rows = pl.ds(pl.multiple_of(sub * band, band), band)
    flux[...] = factor[rows, :] * (sst[...] - held[:, levels - 1, :])
    for copy in copies:
        copy.wait()


def ocean_kernel(
    width, n_sub, place, ids, flux, from_east_flux, weights, temp_in, diffusivity, mask_in, inverse,
    from_west, from_east, even_rows, odd_rows, folded, out, window, picked, sems,
):
    sub = place[0]
    band = flux.shape[0]
    entries = picked.shape[0]
    picks = [
        pltpu.make_async_copy(weights.at[ids[entries + i]], picked.at[i], sems.at[i])
        for i in range(entries)
    ]
    for pick in picks:
        pick.start()
    for side, source in enumerate((flux, from_east_flux)):
        for g in range(2):
            at = (side * 2 + g) * band
            window[at : at + band, :] = source[:, g * LANES : (g + 1) * LANES]
    levels, rows, cells = temp_in.shape
    temp = temp_in[...]
    mask = mask_in[...].astype(F32)
    even = lax.rem(sub, 2) == 0
    own_south = temp[:, 0, :]
    south_row = jnp.where(even, jnp.where(sub == 0, own_south, odd_rows[...]), even_rows[...])
    north_row = jnp.where(
        even, even_rows[...], jnp.where(sub == n_sub - 1, folded[...], odd_rows[...])
    )
    south = jnp.concatenate([south_row[:, None, :], temp[:, :-1, :]], axis=1)
    north = jnp.concatenate([temp[:, 1:, :], north_row[:, None, :]], axis=1)

    def column(message):
        side = message[16:24, :].T
        return jnp.concatenate([side[:, 0:1], side[:, 1:2]], axis=0)

    flat = temp.reshape(levels * rows, cells)
    lane = lax.broadcasted_iota(jnp.int32, flat.shape, 1)
    west = jnp.where(lane == 0, column(from_west), pltpu.roll(flat, 1, 1))
    east = jnp.where(lane == cells - 1, column(from_east), pltpu.roll(flat, cells - 1, 1))
    lap = (west + east).reshape(temp.shape) + north + south - 4.0 * temp
    stepped = mask[None] * (temp + diffusivity[...][None] * lap)
    by_row = jnp.swapaxes(stepped, 0, 1)
    level = lax.broadcasted_iota(jnp.int32, (levels, cells), 0)
    high, low = split(inverse[...])
    made = []
    for row in range(rows):
        total = jnp.zeros((LANES, LANES), F32)
        for k in range(row * width, (row + 1) * width):
            picks[k].wait()
            total = total + picked[k] * window[pl.ds(ids[k], 1), :]
        heat = mask[row : row + 1, :] * jnp.sum(total.T, axis=0, keepdims=True)
        x_high, x_low = split(by_row[row] + jnp.where(level == 0, heat, 0.0))
        made.append(
            jnp.dot(high, x_high, preferred_element_type=F32)
            + jnp.dot(high, x_low, preferred_element_type=F32)
            + jnp.dot(low, x_high, preferred_element_type=F32)
        )
    out[...] = jnp.swapaxes(jnp.stack(made), 0, 1)


def place_kernel(parts, out, sems):
    bands, pieces, _, step, _ = parts.shape
    copies = []
    for band in range(bands):
        for piece in range(pieces):
            at = band * pieces + piece
            rows = pl.ds(at * step, step)
            copies.append(pltpu.make_async_copy(parts.at[band, piece], out.at[:, rows, :], sems.at[at]))
            copies[-1].start()
    for copy in copies:
        copy.wait()


def pair_exchanges(n_lon, n_sub):
    first, second = [], []
    for lon in range(n_lon):
        at = lon * n_sub
        for south in range(n_sub - 1):
            pairs = first if south % 2 == 0 else second
            pairs += [(at + south, at + south + 1), (at + south + 1, at + south)]
        second.append((at + n_sub - 1, (n_lon - 1 - lon) * n_sub + n_sub - 1))
    return first, second


def per_device(
    atm_tracer,
    courant,
    column_inverse,
    heat_exchange_factor,
    ocean_temp,
    diffusivity,
    ocean_inverse,
    land_mask,
    weights,
    a2o_src,
    a2o_wgt,
    o2a_src,
    o2a_wgt,
):
    lon_index = lax.axis_index("lon")
    sub_index = lax.axis_index("sub")
    n_lon = lax.axis_size("lon")
    n_sub = lax.axis_size("sub")
    lev_dev, alat, alon_dev = atm_tracer.shape
    groups = alon_dev // LANES
    ngroups = groups * n_lon
    olev, olat_dev, olon_dev = ocean_temp.shape
    aband = alat // n_sub
    width = o2a_src.shape[2]
    ocean_flat = ocean_temp.reshape(olev * olat_dev, olon_dev)
    place = jnp.reshape(sub_index, (1,))

    east_msg, west_msg, atm_here = kernel_call(
        edges_kernel, (shape(32, LANES), shape(24, LANES), in_vmem(lev_dev, alat, alon_dev)), [HBM] * 3, (VMEM,) * 3,
        scratch=[
            pltpu.VMEM(ocean_flat.shape, F32), pltpu.VMEM(land_mask.shape, land_mask.dtype),
            pltpu.SemaphoreType.DMA((PIECES + 2,)),
        ],
        flops=2 * MIB, moved=2 * MIB, name="edges",
    )(stays(atm_tracer), stays(ocean_flat), stays(land_mask))
    up = [(i, (i + 1) % n_lon) for i in range(n_lon)]
    down = [(b, a) for a, b in up]
    from_west = lax.ppermute(east_msg, "lon", up)
    from_east = lax.ppermute(west_msg, "lon", down)

    base, west_speed, east_speed = kernel_call(
        base_kernel,
        (in_vmem(n_sub, aband, lev_dev, alon_dev), shape(lev_dev, LANES), shape(lev_dev, LANES)),
        [VMEM] * 2, (VMEM,) * 3, flops=10 * MIB, moved=6 * MIB, name="base",
    )(atm_here, courant)
    advected = kernel_call(
        inflow_kernel, in_hbm(n_sub, aband, lev_dev, alon_dev), [VMEM] * 5, HBM,
        scratch=[pltpu.VMEM((n_sub, aband, lev_dev, alon_dev), F32), pltpu.SemaphoreType.DMA((n_sub,))],
        flops=2 * MIB, moved=4 * MIB, name="inflow",
    )(base, west_speed, east_speed, from_west, from_east)
    columns = lax.all_to_all(advected, "sub", split_axis=0, concat_axis=0, tiled=True)

    band_src = lax.dynamic_slice_in_dim(o2a_src, sub_index * aband, aband, 0).reshape(-1)
    band_wgt = lax.dynamic_slice_in_dim(o2a_wgt, sub_index * aband, aband, 0).reshape(-1)
    tile = jnp.remainder(band_src % n_lon - lon_index + 1, n_lon)
    sea_ids = tile * olat_dev + band_src // n_lon - sub_index * olat_dev
    sst, even_msg, odd_msg = kernel_call(
        functools.partial(sst_kernel, width),
        (shape(aband, alon_dev), shape(olev, LANES), shape(olev, LANES)), [SMEM] * 2 + [VMEM] * 4, (VMEM,) * 3,
        scratch=[pltpu.VMEM((2 * olat_dev, LANES), F32), pltpu.VMEM((groups, aband, LANES), F32)],
        flops=8 * MIB, moved=8 * MIB, name="sst",
    )(place, jnp.concatenate([sea_ids, band_wgt]), from_west, ocean_flat, land_mask, weights)
    first, second = pair_exchanges(n_lon, n_sub)
    even_rows = lax.ppermute(even_msg, ("lon", "sub"), first)
    odd_rows = lax.ppermute(odd_msg, ("lon", "sub"), second)
    folded = jnp.flip(odd_rows, axis=1)

    step = 8
    halves = aband // step
    solved, flux_band = kernel_call(
        solve_kernel, (in_hbm(n_sub, halves, lev_dev, step, alon_dev), shape(aband, alon_dev)),
        [SMEM] + [VMEM] * 4 + [ANY] * 2, (HBM, VMEM),
        scratch=[
            pltpu.VMEM((aband, lev_dev * n_sub, alon_dev), F32),
            pltpu.VMEM((n_sub, halves, lev_dev, step, alon_dev), F32), pltpu.SemaphoreType.DMA((n_sub * halves,)),
        ],
        flops=400 * MIB, moved=4 * MIB, name="solve",
    )(place, columns, column_inverse, heat_exchange_factor, sst, even_rows, odd_rows)
    parts = lax.all_to_all(solved, "sub", split_axis=0, concat_axis=0, tiled=True)
    east_flux = lax.ppermute(flux_band, "lon", down)

    src = a2o_src.reshape(-1)
    group = jnp.remainder(src % ngroups - lon_index * groups, ngroups)
    flux_ids = group * aband + src // ngroups - sub_index * aband
    entries = src.shape[0]
    ocean_new = kernel_call(
        functools.partial(ocean_kernel, width, n_sub), shape(olev, olat_dev, olon_dev),
        [SMEM] * 2 + [VMEM] * 2 + [HBM] + [VMEM] * 9, VMEM,
        scratch=[
            pltpu.VMEM((4 * aband, LANES), F32), pltpu.VMEM((entries, LANES, LANES), F32),
            pltpu.SemaphoreType.DMA((entries,)),
        ],
        flops=8 * MIB, moved=4 * MIB, name="ocean",
    )(
        place, jnp.concatenate([flux_ids, a2o_wgt.reshape(-1)]), flux_band, east_flux, stays(weights),
        ocean_temp, diffusivity, land_mask, ocean_inverse, from_west, from_east, even_rows, odd_rows, folded,
    )
    returned = kernel_call(
        place_kernel, shape(lev_dev, alat, alon_dev), [VMEM], HBM,
        scratch=[pltpu.SemaphoreType.DMA((n_sub * halves,))], moved=4 * MIB, name="place",
    )(parts)
    return returned, ocean_new, flux_band


def solution(mesh):
    return jax.shard_map(
        per_device,
        mesh=mesh,
        in_specs=(
            P("sub", None, "lon"),
            P("sub", None, "lon"),
            P(),
            P(None, "lon"),
            P(None, "sub", "lon"),
            P("sub", "lon"),
            P(),
            P("sub", "lon"),
            P(),
            P("sub", "lon", None),
            P("sub", "lon", None),
            P(None, "lon", None),
            P(None, "lon", None),
        ),
        out_specs=(P("sub", None, "lon"), P(None, "sub", "lon"), P("sub", "lon")),
        check_vma=False,
    )
```

```python
import functools

import jax
import jax.numpy as jnp
from jax import lax
from jax.experimental import pallas as pl
from jax.experimental.pallas import tpu as pltpu
from jax.sharding import PartitionSpec as P

F32 = jnp.float32
BF16 = jnp.bfloat16
VMEM = pl.BlockSpec(memory_space=pltpu.VMEM)
SMEM = pl.BlockSpec(memory_space=pltpu.SMEM)
ANY = pl.BlockSpec(memory_space=pl.ANY)
MIB = 1 << 20
LANES = 128
PIECES = 4
HBM = pl.BlockSpec(memory_space=pltpu.HBM)


def kernel_call(body, out_shape, in_specs, out_specs, scratch=(), flops=0, moved=0, limit=16, name=None):
    return pl.pallas_call(
        body,
        out_shape=out_shape,
        in_specs=in_specs,
        out_specs=out_specs,
        scratch_shapes=list(scratch),
        compiler_params=pltpu.CompilerParams(vmem_limit_bytes=limit * MIB),
        cost_estimate=pl.CostEstimate(flops=flops, bytes_accessed=moved, transcendentals=0),
        name=name,
    )


def shape(*dims):
    return jax.ShapeDtypeStruct(dims, F32)


def in_hbm(*dims):
    return pltpu.HBM(dims, F32)


def in_vmem(*dims):
    return pltpu.VMEM(dims, F32)


def stays(value):
    return pltpu.with_memory_space_constraint(value, pltpu.HBM)


def split(value):
    high = value.astype(BF16)
    return high, (value - high.astype(F32)).astype(BF16)


def edges_kernel(place, atm_in, ocean_in, mask_in, east_msg, west_msg, even_msg, odd_msg, atm, ocean, mask, sems):
    levels, rows, cells = atm.shape
    step = levels // PIECES
    pieces = [pl.ds(piece * step, step) for piece in range(PIECES)]
    copies = [pltpu.make_async_copy(atm_in.at[p], atm.at[p], sems.at[i]) for i, p in enumerate(pieces)]
    copies.append(pltpu.make_async_copy(ocean_in, ocean, sems.at[PIECES]))
    copies.append(pltpu.make_async_copy(mask_in, mask, sems.at[PIECES + 1]))
    for copy in copies:
        copy.start()
    lane = lax.broadcasted_iota(jnp.int32, (LANES, LANES), 1)
    last = jnp.zeros((LANES, LANES), F32)
    first = jnp.zeros((LANES, LANES), F32)

    def gather(at, low, high, first, last):
        turned = pltpu.roll(jnp.where(lane == LANES - 1, high, low), at, 1)
        return (
            jnp.where(lane == at, turned, first),
            jnp.where(lane == (at + LANES - 1) % LANES, turned, last),
        )

    for piece in range(PIECES):
        copies[piece].wait()
        for level in range(piece * step, (piece + 1) * step):
            first, last = gather(
                level, atm[level, :, :LANES], atm[level, :, cells - LANES :], first, last
            )
    for copy in copies[PIECES:]:
        copy.wait()
    for part in range(2):
        tile = ocean[part * LANES : (part + 1) * LANES, :]
        first, last = gather(levels + part, tile, tile, first, last)
    last = pltpu.roll(last, 1, 1)
    east_msg[:24, :] = last.T[:24, :]
    east_msg[24:, :] = mask[...].astype(F32) * ocean[:8, :]
    west_msg[...] = first.T[:24, :]
    tile_rows = mask.shape[0]
    tile = ocean[...].reshape(-1, tile_rows, LANES)
    even = lax.rem(place[0], 2) == 0
    low, top = tile[:, 0, :], tile[:, tile_rows - 1, :]
    even_msg[...] = jnp.where(even, top, low)
    odd_msg[...] = jnp.where(even, low, top)


def base_kernel(atm, courant, out, west_speed, east_speed):
    levels, _, cells = atm.shape
    band = out.shape[1]
    lane = lax.broadcasted_iota(jnp.int32, (band, cells), 1)

    @pl.loop(0, out.shape[0])
    def _(dest):
        rows = pl.ds(pl.multiple_of(dest * band, band), band)
        made = []
        for level in range(levels):
            here = atm[level, rows, :]
            speed = courant[level, rows, :]
            west = jnp.where(lane == 0, 0.0, pltpu.roll(here, 1, 1))
            east = jnp.where(lane == cells - 1, 0.0, pltpu.roll(here, cells - 1, 1))
            made.append(
                here
                - jnp.maximum(speed, 0.0) * (here - west)
                - jnp.minimum(speed, 0.0) * (east - here)
            )
        out[dest] = jnp.swapaxes(jnp.stack(made), 0, 1)

    at = lax.broadcasted_iota(jnp.int32, (LANES, LANES), 1)
    first = jnp.zeros((LANES, LANES), F32)
    last = jnp.zeros((LANES, LANES), F32)
    for level in range(levels):
        first = jnp.where(at == level, courant[level, :, 0:1], first)
        last = jnp.where(at == level, courant[level, :, cells - 1 : cells], last)
    west_speed[...] = jnp.maximum(first.T[:levels, :], 0.0)
    east_speed[...] = jnp.minimum(last.T[:levels, :], 0.0)


def inflow_kernel(base, west_speed, east_speed, from_west, from_east, out, held, sems):
    dests, band, levels, cells = base.shape
    west = west_speed[...] * from_west[:levels, :]
    east = -east_speed[...] * from_east[:levels, :]
    lane = lax.broadcasted_iota(jnp.int32, (levels, LANES), 1)
    copies = []
    for dest in range(dests):
        for row in range(band):
            at = dest * band + row
            held[dest, row, :, :LANES] = base[dest, row, :, :LANES] + jnp.where(
                lane == 0, west[:, at : at + 1], 0.0
            )
            held[dest, row, :, cells - LANES :] = base[dest, row, :, cells - LANES :] + jnp.where(
                lane == LANES - 1, east[:, at : at + 1], 0.0
            )
        copies.append(pltpu.make_async_copy(held.at[dest], out.at[dest], sems.at[dest]))
        copies[-1].start()
    for copy in copies:
        copy.wait()


def mat_vec(ids, first, count, source, weights):
    total = jnp.zeros(weights.shape[1:], F32)
    half = ids.shape[0] // 2
    for k in range(count):
        block = source[pl.ds(ids[first + k], 1), :]
        total = total + weights[ids[half + first + k]] * block
    return jnp.sum(total.T, axis=0, keepdims=True)


def sst_kernel(width, ids, from_west, ocean, mask, weights, sst, window, halves):
    window[:8, :] = from_west[24:32, :]
    window[8:, :] = mask[...].astype(F32) * ocean[:8, :]
    rows = sst.shape[0]

    @pl.loop(0, rows)
    def _(row):
        for g in range(2):
            halves[g, pl.ds(row, 1), :] = mat_vec(ids, (row * 2 + g) * width, width, window, weights)

    for g in range(2):
        sst[:, g * LANES : (g + 1) * LANES] = halves[g]


def solve_kernel(place, columns, inverse, factor, sst, out, flux, held, turned, sems):
    sub = place[0]
    groups, band, depth, cells = columns.shape
    levels = groups * depth
    parts, step = out.shape[1], out.shape[3]
    high, low = split(inverse[sub])
    thrice = jnp.concatenate([high, high, low], axis=1)
    copies = []
    for part in range(parts):
        for row in range(part * step, (part + 1) * step):
            x_high, x_low = split(columns[:, row].reshape(levels, cells))
            held[row] = jnp.dot(
                thrice, jnp.concatenate([x_high, x_low, x_high], axis=0), preferred_element_type=F32
            )
        for group in range(groups):
            turned[group, part] = jnp.swapaxes(
                held[part * step : (part + 1) * step, group * depth : (group + 1) * depth, :], 0, 1
            )
            copies.append(
                pltpu.make_async_copy(
                    turned.at[group, part], out.at[group, part], sems.at[group * parts + part]
                )
            )
            copies[-1].start()
    rows = pl.ds(pl.multiple_of(sub * band, band), band)
    flux[...] = factor[rows, :] * (sst[...] - held[:, levels - 1, :])
    for copy in copies:
        copy.wait()


def ocean_kernel(
    width, n_sub, place, ids, flux, from_east_flux, weights, temp_in, diffusivity, mask_in, inverse,
    from_west, from_east, even_rows, odd_rows, folded, out, window, picked, sems,
):
    sub = place[0]
    band = flux.shape[0]
    entries = picked.shape[0]
    picks = [
        pltpu.make_async_copy(weights.at[ids[entries + i]], picked.at[i], sems.at[i])
        for i in range(entries)
    ]
    for pick in picks:
        pick.start()
    for side, source in enumerate((flux, from_east_flux)):
        for g in range(2):
            at = (side * 2 + g) * band
            window[at : at + band, :] = source[:, g * LANES : (g + 1) * LANES]
    levels, rows, cells = temp_in.shape
    temp = temp_in[...]
    mask = mask_in[...].astype(F32)
    even = lax.rem(sub, 2) == 0
    own_south = temp[:, 0, :]
    south_row = jnp.where(even, jnp.where(sub == 0, own_south, odd_rows[...]), even_rows[...])
    north_row = jnp.where(
        even, even_rows[...], jnp.where(sub == n_sub - 1, folded[...], odd_rows[...])
    )
    south = jnp.concatenate([south_row[:, None, :], temp[:, :-1, :]], axis=1)
    north = jnp.concatenate([temp[:, 1:, :], north_row[:, None, :]], axis=1)

    def column(message):
        side = message[16:24, :].T
        return jnp.concatenate([side[:, 0:1], side[:, 1:2]], axis=0)

    flat = temp.reshape(levels * rows, cells)
    lane = lax.broadcasted_iota(jnp.int32, flat.shape, 1)
    west = jnp.where(lane == 0, column(from_west), pltpu.roll(flat, 1, 1))
    east = jnp.where(lane == cells - 1, column(from_east), pltpu.roll(flat, cells - 1, 1))
    lap = (west + east).reshape(temp.shape) + north + south - 4.0 * temp
    stepped = mask[None] * (temp + diffusivity[...][None] * lap)
    by_row = jnp.swapaxes(stepped, 0, 1)
    level = lax.broadcasted_iota(jnp.int32, (levels, cells), 0)
    high, low = split(inverse[...])
    made = []
    for row in range(rows):
        total = jnp.zeros((LANES, LANES), F32)
        for k in range(row * width, (row + 1) * width):
            picks[k].wait()
            total = total + picked[k] * window[pl.ds(ids[k], 1), :]
        heat = mask[row : row + 1, :] * jnp.sum(total.T, axis=0, keepdims=True)
        x_high, x_low = split(by_row[row] + jnp.where(level == 0, heat, 0.0))
        made.append(
            jnp.dot(high, x_high, preferred_element_type=F32)
            + jnp.dot(high, x_low, preferred_element_type=F32)
            + jnp.dot(low, x_high, preferred_element_type=F32)
        )
    out[...] = jnp.swapaxes(jnp.stack(made), 0, 1)


def place_kernel(parts, out, sems):
    bands, pieces, _, step, _ = parts.shape
    copies = []
    for band in range(bands):
        for piece in range(pieces):
            at = band * pieces + piece
            rows = pl.ds(at * step, step)
            copies.append(pltpu.make_async_copy(parts.at[band, piece], out.at[:, rows, :], sems.at[at]))
            copies[-1].start()
    for copy in copies:
        copy.wait()


def pair_exchanges(n_lon, n_sub):
    first, second = [], []
    for lon in range(n_lon):
        at = lon * n_sub
        for south in range(n_sub - 1):
            pairs = first if south % 2 == 0 else second
            pairs += [(at + south, at + south + 1), (at + south + 1, at + south)]
        second.append((at + n_sub - 1, (n_lon - 1 - lon) * n_sub + n_sub - 1))
    return first, second


def per_device(
    atm_tracer,
    courant,
    column_inverse,
    heat_exchange_factor,
    ocean_temp,
    diffusivity,
    ocean_inverse,
    land_mask,
    weights,
    a2o_src,
    a2o_wgt,
    o2a_src,
    o2a_wgt,
):
    lon_index = lax.axis_index("lon")
    sub_index = lax.axis_index("sub")
    n_lon = lax.axis_size("lon")
    n_sub = lax.axis_size("sub")
    lev_dev, alat, alon_dev = atm_tracer.shape
    groups = alon_dev // LANES
    ngroups = groups * n_lon
    olev, olat_dev, olon_dev = ocean_temp.shape
    aband = alat // n_sub
    width = o2a_src.shape[2]
    ocean_flat = ocean_temp.reshape(olev * olat_dev, olon_dev)
    place = jnp.reshape(sub_index, (1,))

    east_msg, west_msg, even_msg, odd_msg, atm_here = kernel_call(
        edges_kernel,
        (shape(32, LANES), shape(24, LANES), shape(olev, LANES), shape(olev, LANES), in_vmem(lev_dev, alat, alon_dev)),
        [SMEM] + [HBM] * 3, (VMEM,) * 5,
        scratch=[
            pltpu.VMEM(ocean_flat.shape, F32), pltpu.VMEM(land_mask.shape, land_mask.dtype),
            pltpu.SemaphoreType.DMA((PIECES + 2,)),
        ],
        flops=2 * MIB, moved=2 * MIB, name="edges",
    )(place, stays(atm_tracer), stays(ocean_flat), stays(land_mask))
    up = [(i, (i + 1) % n_lon) for i in range(n_lon)]
    down = [(b, a) for a, b in up]
    from_west = lax.ppermute(east_msg, "lon", up)
    from_east = lax.ppermute(west_msg, "lon", down)

    first, second = pair_exchanges(n_lon, n_sub)
    even_rows = lax.ppermute(even_msg, ("lon", "sub"), first)
    odd_rows = lax.ppermute(odd_msg, ("lon", "sub"), second)

    base, west_speed, east_speed = kernel_call(
        base_kernel,
        (in_vmem(n_sub, aband, lev_dev, alon_dev), shape(lev_dev, LANES), shape(lev_dev, LANES)),
        [VMEM] * 2, (VMEM,) * 3, flops=10 * MIB, moved=6 * MIB, name="base",
    )(atm_here, courant)
    advected = kernel_call(
        inflow_kernel, in_hbm(n_sub, aband, lev_dev, alon_dev), [VMEM] * 5, HBM,
        scratch=[pltpu.VMEM((n_sub, aband, lev_dev, alon_dev), F32), pltpu.SemaphoreType.DMA((n_sub,))],
        flops=2 * MIB, moved=4 * MIB, name="inflow",
    )(base, west_speed, east_speed, from_west, from_east)
    columns = lax.all_to_all(advected, "sub", split_axis=0, concat_axis=0, tiled=True)

    band_src = lax.dynamic_slice_in_dim(o2a_src, sub_index * aband, aband, 0).reshape(-1)
    band_wgt = lax.dynamic_slice_in_dim(o2a_wgt, sub_index * aband, aband, 0).reshape(-1)
    tile = jnp.remainder(band_src % n_lon - lon_index + 1, n_lon)
    sea_ids = tile * olat_dev + band_src // n_lon - sub_index * olat_dev
    sst = kernel_call(
        functools.partial(sst_kernel, width), shape(aband, alon_dev), [SMEM] + [VMEM] * 4, VMEM,
        scratch=[pltpu.VMEM((2 * olat_dev, LANES), F32), pltpu.VMEM((groups, aband, LANES), F32)],
        flops=8 * MIB, moved=8 * MIB, name="sst",
    )(jnp.concatenate([sea_ids, band_wgt]), from_west, ocean_flat, land_mask, weights)
    step = 8
    halves = aband // step
    solved, flux_band = kernel_call(
        solve_kernel, (in_hbm(n_sub, halves, lev_dev, step, alon_dev), shape(aband, alon_dev)),
        [SMEM] + [VMEM] * 4, (HBM, VMEM),
        scratch=[
            pltpu.VMEM((aband, lev_dev * n_sub, alon_dev), F32),
            pltpu.VMEM((n_sub, halves, lev_dev, step, alon_dev), F32), pltpu.SemaphoreType.DMA((n_sub * halves,)),
        ],
        flops=400 * MIB, moved=4 * MIB, name="solve",
    )(place, columns, column_inverse, heat_exchange_factor, sst)
    solved, even_rows, odd_rows = lax.optimization_barrier((solved, even_rows, odd_rows))
    folded = jnp.flip(odd_rows, axis=1)
    parts = lax.all_to_all(solved, "sub", split_axis=0, concat_axis=0, tiled=True)
    east_flux = lax.ppermute(flux_band, "lon", down)

    src = a2o_src.reshape(-1)
    group = jnp.remainder(src % ngroups - lon_index * groups, ngroups)
    flux_ids = group * aband + src // ngroups - sub_index * aband
    entries = src.shape[0]
    ocean_new = kernel_call(
        functools.partial(ocean_kernel, width, n_sub), shape(olev, olat_dev, olon_dev),
        [SMEM] * 2 + [VMEM] * 2 + [HBM] + [VMEM] * 9, VMEM,
        scratch=[
            pltpu.VMEM((4 * aband, LANES), F32), pltpu.VMEM((entries, LANES, LANES), F32),
            pltpu.SemaphoreType.DMA((entries,)),
        ],
        flops=8 * MIB, moved=4 * MIB, name="ocean",
    )(
        place, jnp.concatenate([flux_ids, a2o_wgt.reshape(-1)]), flux_band, east_flux, stays(weights),
        ocean_temp, diffusivity, land_mask, ocean_inverse, from_west, from_east, even_rows, odd_rows, folded,
    )
    returned = kernel_call(
        place_kernel, shape(lev_dev, alat, alon_dev), [VMEM], HBM,
        scratch=[pltpu.SemaphoreType.DMA((n_sub * halves,))], moved=4 * MIB, name="place",
    )(parts)
    return returned, ocean_new, flux_band


def solution(mesh):
    return jax.shard_map(
        per_device,
        mesh=mesh,
        in_specs=(
            P("sub", None, "lon"),
            P("sub", None, "lon"),
            P(),
            P(None, "lon"),
            P(None, "sub", "lon"),
            P("sub", "lon"),
            P(),
            P("sub", "lon"),
            P(),
            P("sub", "lon", None),
            P("sub", "lon", None),
            P(None, "lon", None),
            P(None, "lon", None),
        ),
        out_specs=(P("sub", None, "lon"), P(None, "sub", "lon"), P("sub", "lon")),
        check_vma=False,
    )
```

```python
import functools

import jax
import jax.numpy as jnp
from jax import lax
from jax.experimental import pallas as pl
from jax.experimental.pallas import tpu as pltpu
from jax.sharding import PartitionSpec as P

F32 = jnp.float32
BF16 = jnp.bfloat16
VMEM = pl.BlockSpec(memory_space=pltpu.VMEM)
SMEM = pl.BlockSpec(memory_space=pltpu.SMEM)
ANY = pl.BlockSpec(memory_space=pl.ANY)
MIB = 1 << 20
LANES = 128
PIECES = 4
HBM = pl.BlockSpec(memory_space=pltpu.HBM)


def kernel_call(body, out_shape, in_specs, out_specs, scratch=(), flops=0, moved=0, limit=16, name=None):
    return pl.pallas_call(
        body,
        out_shape=out_shape,
        in_specs=in_specs,
        out_specs=out_specs,
        scratch_shapes=list(scratch),
        compiler_params=pltpu.CompilerParams(vmem_limit_bytes=limit * MIB),
        cost_estimate=pl.CostEstimate(flops=flops, bytes_accessed=moved, transcendentals=0),
        name=name,
    )


def shape(*dims):
    return jax.ShapeDtypeStruct(dims, F32)


def in_hbm(*dims):
    return pltpu.HBM(dims, F32)


def in_vmem(*dims):
    return pltpu.VMEM(dims, F32)


def stays(value):
    return pltpu.with_memory_space_constraint(value, pltpu.HBM)


def split(value):
    high = value.astype(BF16)
    return high, (value - high.astype(F32)).astype(BF16)


def gather(lane, at, low, high, first, last):
    turned = pltpu.roll(jnp.where(lane == LANES - 1, high, low), at, 1)
    return (
        jnp.where(lane == at, turned, first),
        jnp.where(lane == (at + LANES - 1) % LANES, turned, last),
    )


def edges_kernel(place, atm_in, ocean_in, mask_in, east_msg, west_msg, even_msg, odd_msg, atm, ocean, mask, sems):
    levels, rows, cells = atm.shape
    step = levels // PIECES
    pieces = [pl.ds(piece * step, step) for piece in range(PIECES)]
    copies = [pltpu.make_async_copy(atm_in.at[p], atm.at[p], sems.at[i]) for i, p in enumerate(pieces)]
    copies.append(pltpu.make_async_copy(ocean_in, ocean, sems.at[PIECES]))
    copies.append(pltpu.make_async_copy(mask_in, mask, sems.at[PIECES + 1]))
    for copy in copies:
        copy.start()
    lane = lax.broadcasted_iota(jnp.int32, (LANES, LANES), 1)
    last = jnp.zeros((LANES, LANES), F32)
    first = jnp.zeros((LANES, LANES), F32)

    for piece in range(PIECES):
        copies[piece].wait()
        for level in range(piece * step, (piece + 1) * step):
            first, last = gather(
                lane, level, atm[level, :, :LANES], atm[level, :, cells - LANES :], first, last
            )
    for copy in copies[PIECES:]:
        copy.wait()
    for part in range(2):
        tile = ocean[part * LANES : (part + 1) * LANES, :]
        first, last = gather(lane, levels + part, tile, tile, first, last)
    last = pltpu.roll(last, 1, 1)
    east_msg[:24, :] = last.T[:24, :]
    east_msg[24:, :] = mask[...].astype(F32) * ocean[:8, :]
    west_msg[...] = first.T[:24, :]
    tile_rows = mask.shape[0]
    tile = ocean[...].reshape(-1, tile_rows, LANES)
    even = lax.rem(place[0], 2) == 0
    low, top = tile[:, 0, :], tile[:, tile_rows - 1, :]
    even_msg[...] = jnp.where(even, top, low)
    odd_msg[...] = jnp.where(even, low, top)


def base_kernel(atm, courant, out, west_speed, east_speed):
    levels, _, cells = atm.shape
    band = out.shape[1]
    lane = lax.broadcasted_iota(jnp.int32, (band, cells), 1)

    @pl.loop(0, out.shape[0])
    def _(dest):
        rows = pl.ds(pl.multiple_of(dest * band, band), band)
        made = []
        for level in range(levels):
            here = atm[level, rows, :]
            speed = courant[level, rows, :]
            west = jnp.where(lane == 0, 0.0, pltpu.roll(here, 1, 1))
            east = jnp.where(lane == cells - 1, 0.0, pltpu.roll(here, cells - 1, 1))
            made.append(
                here
                - jnp.maximum(speed, 0.0) * (here - west)
                - jnp.minimum(speed, 0.0) * (east - here)
            )
        out[dest] = jnp.swapaxes(jnp.stack(made), 0, 1)

    at = lax.broadcasted_iota(jnp.int32, (LANES, LANES), 1)
    first = jnp.zeros((LANES, LANES), F32)
    last = jnp.zeros((LANES, LANES), F32)
    for level in range(levels):
        first, last = gather(at, level, courant[level, :, :LANES], courant[level, :, cells - LANES :], first, last)
    last = pltpu.roll(last, 1, 1)
    west_speed[...] = jnp.maximum(first.T[:levels, :], 0.0)
    east_speed[...] = jnp.minimum(last.T[:levels, :], 0.0)


def inflow_kernel(base, west_speed, east_speed, from_west, from_east, out, held, sems):
    dests, band, levels, cells = base.shape
    west = west_speed[...] * from_west[:levels, :]
    east = -east_speed[...] * from_east[:levels, :]
    lane = lax.broadcasted_iota(jnp.int32, (levels, LANES), 1)
    copies = []
    for dest in range(dests):
        for row in range(band):
            at = dest * band + row
            held[dest, row, :, :LANES] = base[dest, row, :, :LANES] + jnp.where(
                lane == 0, west[:, at : at + 1], 0.0
            )
            held[dest, row, :, cells - LANES :] = base[dest, row, :, cells - LANES :] + jnp.where(
                lane == LANES - 1, east[:, at : at + 1], 0.0
            )
        copies.append(pltpu.make_async_copy(held.at[dest], out.at[dest], sems.at[dest]))
        copies[-1].start()
    for copy in copies:
        copy.wait()


def mat_vec(ids, first, count, source, weights):
    total = jnp.zeros(weights.shape[1:], F32)
    half = ids.shape[0] // 2
    for k in range(count):
        block = source[pl.ds(ids[first + k], 1), :]
        total = total + weights[ids[half + first + k]] * block
    return jnp.sum(total.T, axis=0, keepdims=True)


def sst_kernel(width, ids, from_west, ocean, mask, weights, sst, window, halves):
    window[:8, :] = from_west[24:32, :]
    window[8:, :] = mask[...].astype(F32) * ocean[:8, :]
    rows = sst.shape[0]

    @pl.loop(0, rows)
    def _(row):
        for g in range(2):
            halves[g, pl.ds(row, 1), :] = mat_vec(ids, (row * 2 + g) * width, width, window, weights)

    for g in range(2):
        sst[:, g * LANES : (g + 1) * LANES] = halves[g]


def solve_kernel(place, columns, inverse, factor, sst, out, flux, held, turned, sems):
    sub = place[0]
    groups, band, depth, cells = columns.shape
    levels = groups * depth
    parts, step = out.shape[1], out.shape[3]
    high, low = split(inverse[sub])
    thrice = jnp.concatenate([high, high, low], axis=1)
    copies = []
    for part in range(parts):
        for row in range(part * step, (part + 1) * step):
            x_high, x_low = split(columns[:, row].reshape(levels, cells))
            held[row] = jnp.dot(
                thrice, jnp.concatenate([x_high, x_low, x_high], axis=0), preferred_element_type=F32
            )
        for group in range(groups):
            turned[group, part] = jnp.swapaxes(
                held[part * step : (part + 1) * step, group * depth : (group + 1) * depth, :], 0, 1
            )
            copies.append(
                pltpu.make_async_copy(
                    turned.at[group, part], out.at[group, part], sems.at[group * parts + part]
                )
            )
            copies[-1].start()
    rows = pl.ds(pl.multiple_of(sub * band, band), band)
    flux[...] = factor[rows, :] * (sst[...] - held[:, levels - 1, :])
    for copy in copies:
        copy.wait()


def ocean_kernel(
    width, n_sub, place, ids, flux, from_east_flux, weights, temp_in, diffusivity, mask_in, inverse,
    from_west, from_east, even_rows, odd_rows, folded, out, window, picked, sems,
):
    sub = place[0]
    band = flux.shape[0]
    entries = picked.shape[0]
    picks = [
        pltpu.make_async_copy(weights.at[ids[entries + i]], picked.at[i], sems.at[i])
        for i in range(entries)
    ]
    for pick in picks:
        pick.start()
    for side, source in enumerate((flux, from_east_flux)):
        for g in range(2):
            at = (side * 2 + g) * band
            window[at : at + band, :] = source[:, g * LANES : (g + 1) * LANES]
    levels, rows, cells = temp_in.shape
    temp = temp_in[...]
    mask = mask_in[...].astype(F32)
    even = lax.rem(sub, 2) == 0
    own_south = temp[:, 0, :]
    south_row = jnp.where(even, jnp.where(sub == 0, own_south, odd_rows[...]), even_rows[...])
    north_row = jnp.where(
        even, even_rows[...], jnp.where(sub == n_sub - 1, folded[...], odd_rows[...])
    )
    south = jnp.concatenate([south_row[:, None, :], temp[:, :-1, :]], axis=1)
    north = jnp.concatenate([temp[:, 1:, :], north_row[:, None, :]], axis=1)

    def column(message):
        side = message[16:24, :].T
        return jnp.concatenate([side[:, 0:1], side[:, 1:2]], axis=0)

    flat = temp.reshape(levels * rows, cells)
    lane = lax.broadcasted_iota(jnp.int32, flat.shape, 1)
    west = jnp.where(lane == 0, column(from_west), pltpu.roll(flat, 1, 1))
    east = jnp.where(lane == cells - 1, column(from_east), pltpu.roll(flat, cells - 1, 1))
    lap = (west + east).reshape(temp.shape) + north + south - 4.0 * temp
    stepped = mask[None] * (temp + diffusivity[...][None] * lap)
    by_row = jnp.swapaxes(stepped, 0, 1)
    level = lax.broadcasted_iota(jnp.int32, (levels, cells), 0)
    high, low = split(inverse[...])
    made = []
    for row in range(rows):
        total = jnp.zeros((LANES, LANES), F32)
        for k in range(row * width, (row + 1) * width):
            picks[k].wait()
            total = total + picked[k] * window[pl.ds(ids[k], 1), :]
        heat = mask[row : row + 1, :] * jnp.sum(total.T, axis=0, keepdims=True)
        x_high, x_low = split(by_row[row] + jnp.where(level == 0, heat, 0.0))
        made.append(
            jnp.dot(high, x_high, preferred_element_type=F32)
            + jnp.dot(high, x_low, preferred_element_type=F32)
            + jnp.dot(low, x_high, preferred_element_type=F32)
        )
    out[...] = jnp.swapaxes(jnp.stack(made), 0, 1)


def place_kernel(parts, out, sems):
    bands, pieces, _, step, _ = parts.shape
    copies = []
    for band in range(bands):
        for piece in range(pieces):
            at = band * pieces + piece
            rows = pl.ds(at * step, step)
            copies.append(pltpu.make_async_copy(parts.at[band, piece], out.at[:, rows, :], sems.at[at]))
            copies[-1].start()
    for copy in copies:
        copy.wait()


def pair_exchanges(n_lon, n_sub):
    first, second = [], []
    for lon in range(n_lon):
        at = lon * n_sub
        for south in range(n_sub - 1):
            pairs = first if south % 2 == 0 else second
            pairs += [(at + south, at + south + 1), (at + south + 1, at + south)]
        second.append((at + n_sub - 1, (n_lon - 1 - lon) * n_sub + n_sub - 1))
    return first, second


def per_device(
    atm_tracer,
    courant,
    column_inverse,
    heat_exchange_factor,
    ocean_temp,
    diffusivity,
    ocean_inverse,
    land_mask,
    weights,
    a2o_src,
    a2o_wgt,
    o2a_src,
    o2a_wgt,
):
    lon_index = lax.axis_index("lon")
    sub_index = lax.axis_index("sub")
    n_lon = lax.axis_size("lon")
    n_sub = lax.axis_size("sub")
    lev_dev, alat, alon_dev = atm_tracer.shape
    groups = alon_dev // LANES
    ngroups = groups * n_lon
    olev, olat_dev, olon_dev = ocean_temp.shape
    aband = alat // n_sub
    width = o2a_src.shape[2]
    ocean_flat = ocean_temp.reshape(olev * olat_dev, olon_dev)
    place = jnp.reshape(sub_index, (1,))

    east_msg, west_msg, even_msg, odd_msg, atm_here = kernel_call(
        edges_kernel,
        (shape(32, LANES), shape(24, LANES), shape(olev, LANES), shape(olev, LANES), in_vmem(lev_dev, alat, alon_dev)),
        [SMEM] + [HBM] * 3, (VMEM,) * 5,
        scratch=[
            pltpu.VMEM(ocean_flat.shape, F32), pltpu.VMEM(land_mask.shape, land_mask.dtype),
            pltpu.SemaphoreType.DMA((PIECES + 2,)),
        ],
        flops=2 * MIB, moved=2 * MIB, name="edges",
    )(place, stays(atm_tracer), stays(ocean_flat), stays(land_mask))
    up = [(i, (i + 1) % n_lon) for i in range(n_lon)]
    down = [(b, a) for a, b in up]
    from_west = lax.ppermute(east_msg, "lon", up)
    from_east = lax.ppermute(west_msg, "lon", down)

    first, second = pair_exchanges(n_lon, n_sub)
    even_rows = lax.ppermute(even_msg, ("lon", "sub"), first)
    odd_rows = lax.ppermute(odd_msg, ("lon", "sub"), second)

    base, west_speed, east_speed = kernel_call(
        base_kernel,
        (in_vmem(n_sub, aband, lev_dev, alon_dev), shape(lev_dev, LANES), shape(lev_dev, LANES)),
        [VMEM] * 2, (VMEM,) * 3, flops=10 * MIB, moved=6 * MIB, name="base",
    )(atm_here, courant)
    advected = kernel_call(
        inflow_kernel, in_hbm(n_sub, aband, lev_dev, alon_dev), [VMEM] * 5, HBM,
        scratch=[pltpu.VMEM((n_sub, aband, lev_dev, alon_dev), F32), pltpu.SemaphoreType.DMA((n_sub,))],
        flops=2 * MIB, moved=4 * MIB, name="inflow",
    )(base, west_speed, east_speed, from_west, from_east)
    columns = lax.all_to_all(advected, "sub", split_axis=0, concat_axis=0, tiled=True)

    band_src = lax.dynamic_slice_in_dim(o2a_src, sub_index * aband, aband, 0).reshape(-1)
    band_wgt = lax.dynamic_slice_in_dim(o2a_wgt, sub_index * aband, aband, 0).reshape(-1)
    tile = jnp.remainder(band_src % n_lon - lon_index + 1, n_lon)
    sea_ids = tile * olat_dev + band_src // n_lon - sub_index * olat_dev
    sst = kernel_call(
        functools.partial(sst_kernel, width), shape(aband, alon_dev), [SMEM] + [VMEM] * 4, VMEM,
        scratch=[pltpu.VMEM((2 * olat_dev, LANES), F32), pltpu.VMEM((groups, aband, LANES), F32)],
        flops=8 * MIB, moved=8 * MIB, name="sst",
    )(jnp.concatenate([sea_ids, band_wgt]), from_west, ocean_flat, land_mask, weights)
    step = 8
    halves = aband // step
    solved, flux_band = kernel_call(
        solve_kernel, (in_hbm(n_sub, halves, lev_dev, step, alon_dev), shape(aband, alon_dev)),
        [SMEM] + [VMEM] * 4, (HBM, VMEM),
        scratch=[
            pltpu.VMEM((aband, lev_dev * n_sub, alon_dev), F32),
            pltpu.VMEM((n_sub, halves, lev_dev, step, alon_dev), F32), pltpu.SemaphoreType.DMA((n_sub * halves,)),
        ],
        flops=400 * MIB, moved=4 * MIB, name="solve",
    )(place, columns, column_inverse, heat_exchange_factor, sst)
    solved, even_rows, odd_rows = lax.optimization_barrier((solved, even_rows, odd_rows))
    folded = jnp.flip(odd_rows, axis=1)
    parts = lax.all_to_all(solved, "sub", split_axis=0, concat_axis=0, tiled=True)
    east_flux = lax.ppermute(flux_band, "lon", down)

    src = a2o_src.reshape(-1)
    group = jnp.remainder(src % ngroups - lon_index * groups, ngroups)
    flux_ids = group * aband + src // ngroups - sub_index * aband
    entries = src.shape[0]
    ocean_new = kernel_call(
        functools.partial(ocean_kernel, width, n_sub), shape(olev, olat_dev, olon_dev),
        [SMEM] * 2 + [VMEM] * 2 + [HBM] + [VMEM] * 9, VMEM,
        scratch=[
            pltpu.VMEM((4 * aband, LANES), F32), pltpu.VMEM((entries, LANES, LANES), F32),
            pltpu.SemaphoreType.DMA((entries,)),
        ],
        flops=8 * MIB, moved=4 * MIB, name="ocean",
    )(
        place, jnp.concatenate([flux_ids, a2o_wgt.reshape(-1)]), flux_band, east_flux, stays(weights),
        ocean_temp, diffusivity, land_mask, ocean_inverse, from_west, from_east, even_rows, odd_rows, folded,
    )
    returned = kernel_call(
        place_kernel, shape(lev_dev, alat, alon_dev), [VMEM], HBM,
        scratch=[pltpu.SemaphoreType.DMA((n_sub * halves,))], moved=4 * MIB, name="place",
    )(parts)
    return returned, ocean_new, flux_band


def solution(mesh):
    return jax.shard_map(
        per_device,
        mesh=mesh,
        in_specs=(
            P("sub", None, "lon"),
            P("sub", None, "lon"),
            P(),
            P(None, "lon"),
            P(None, "sub", "lon"),
            P("sub", "lon"),
            P(),
            P("sub", "lon"),
            P(),
            P("sub", "lon", None),
            P("sub", "lon", None),
            P(None, "lon", None),
            P(None, "lon", None),
        ),
        out_specs=(P("sub", None, "lon"), P(None, "sub", "lon"), P("sub", "lon")),
        check_vma=False,
    )
```

```python
import functools

import jax
import jax.numpy as jnp
from jax import lax
from jax.experimental import pallas as pl
from jax.experimental.pallas import tpu as pltpu
from jax.sharding import PartitionSpec as P

F32 = jnp.float32
BF16 = jnp.bfloat16
VMEM = pl.BlockSpec(memory_space=pltpu.VMEM)
SMEM = pl.BlockSpec(memory_space=pltpu.SMEM)
ANY = pl.BlockSpec(memory_space=pl.ANY)
MIB = 1 << 20
LANES = 128
PIECES = 4
HBM = pl.BlockSpec(memory_space=pltpu.HBM)


def kernel_call(body, out_shape, in_specs, out_specs, scratch=(), flops=0, moved=0, limit=16, name=None):
    return pl.pallas_call(
        body,
        out_shape=out_shape,
        in_specs=in_specs,
        out_specs=out_specs,
        scratch_shapes=list(scratch),
        compiler_params=pltpu.CompilerParams(vmem_limit_bytes=limit * MIB),
        cost_estimate=pl.CostEstimate(flops=flops, bytes_accessed=moved, transcendentals=0),
        name=name,
    )


def shape(*dims):
    return jax.ShapeDtypeStruct(dims, F32)


def in_hbm(*dims):
    return pltpu.HBM(dims, F32)


def in_vmem(*dims):
    return pltpu.VMEM(dims, F32)


def stays(value):
    return pltpu.with_memory_space_constraint(value, pltpu.HBM)


def split(value):
    high = value.astype(BF16)
    return high, (value - high.astype(F32)).astype(BF16)


def gather(lane, at, low, high, first, last):
    turned = pltpu.roll(jnp.where(lane == LANES - 1, high, low), at, 1)
    return (
        jnp.where(lane == at, turned, first),
        jnp.where(lane == (at + LANES - 1) % LANES, turned, last),
    )


def edges_kernel(place, atm_in, ocean_in, mask_in, east_msg, west_msg, even_msg, odd_msg, atm, ocean, mask, sems):
    levels, rows, cells = atm.shape
    step = levels // PIECES
    pieces = [pl.ds(piece * step, step) for piece in range(PIECES)]
    copies = [pltpu.make_async_copy(atm_in.at[p], atm.at[p], sems.at[i]) for i, p in enumerate(pieces)]
    copies.append(pltpu.make_async_copy(ocean_in, ocean, sems.at[PIECES]))
    copies.append(pltpu.make_async_copy(mask_in, mask, sems.at[PIECES + 1]))
    for copy in copies:
        copy.start()
    lane = lax.broadcasted_iota(jnp.int32, (LANES, LANES), 1)
    last = jnp.zeros((LANES, LANES), F32)
    first = jnp.zeros((LANES, LANES), F32)

    for piece in range(PIECES):
        copies[piece].wait()
        for level in range(piece * step, (piece + 1) * step):
            first, last = gather(
                lane, level, atm[level, :, :LANES], atm[level, :, cells - LANES :], first, last
            )
    for copy in copies[PIECES:]:
        copy.wait()
    for part in range(2):
        tile = ocean[part * LANES : (part + 1) * LANES, :]
        first, last = gather(lane, levels + part, tile, tile, first, last)
    last = pltpu.roll(last, 1, 1)
    east_msg[:24, :] = last.T[:24, :]
    east_msg[24:, :] = mask[...].astype(F32) * ocean[:8, :]
    west_msg[...] = first.T[:24, :]
    tile_rows = mask.shape[0]
    tile = ocean[...].reshape(-1, tile_rows, LANES)
    even = lax.rem(place[0], 2) == 0
    low, top = tile[:, 0, :], tile[:, tile_rows - 1, :]
    even_msg[...] = jnp.where(even, top, low)
    odd_msg[...] = jnp.where(even, low, top)


def base_kernel(atm, courant, out, west_speed, east_speed):
    levels, _, cells = atm.shape
    band = out.shape[1]
    lane = lax.broadcasted_iota(jnp.int32, (band, cells), 1)

    @pl.loop(0, out.shape[0], unroll=2)
    def _(dest):
        rows = pl.ds(pl.multiple_of(dest * band, band), band)
        made = []
        for level in range(levels):
            here = atm[level, rows, :]
            speed = courant[level, rows, :]
            west = jnp.where(lane == 0, 0.0, pltpu.roll(here, 1, 1))
            east = jnp.where(lane == cells - 1, 0.0, pltpu.roll(here, cells - 1, 1))
            made.append(
                here
                - jnp.maximum(speed, 0.0) * (here - west)
                - jnp.minimum(speed, 0.0) * (east - here)
            )
        out[dest] = jnp.swapaxes(jnp.stack(made), 0, 1)

    at = lax.broadcasted_iota(jnp.int32, (LANES, LANES), 1)
    first = jnp.zeros((LANES, LANES), F32)
    last = jnp.zeros((LANES, LANES), F32)
    for level in range(levels):
        first, last = gather(at, level, courant[level, :, :LANES], courant[level, :, cells - LANES :], first, last)
    last = pltpu.roll(last, 1, 1)
    west_speed[...] = jnp.maximum(first.T[:levels, :], 0.0)
    east_speed[...] = jnp.minimum(last.T[:levels, :], 0.0)


def inflow_kernel(base, west_speed, east_speed, from_west, from_east, out, held, sems):
    dests, band, levels, cells = base.shape
    west = west_speed[...] * from_west[:levels, :]
    east = -east_speed[...] * from_east[:levels, :]
    lane = lax.broadcasted_iota(jnp.int32, (levels, LANES), 1)
    copies = []
    for dest in range(dests):
        for row in range(band):
            at = dest * band + row
            held[dest, row, :, :LANES] = base[dest, row, :, :LANES] + jnp.where(
                lane == 0, west[:, at : at + 1], 0.0
            )
            held[dest, row, :, cells - LANES :] = base[dest, row, :, cells - LANES :] + jnp.where(
                lane == LANES - 1, east[:, at : at + 1], 0.0
            )
        copies.append(pltpu.make_async_copy(held.at[dest], out.at[dest], sems.at[dest]))
        copies[-1].start()
    for copy in copies:
        copy.wait()


def mat_vec(ids, first, count, source, weights):
    total = jnp.zeros(weights.shape[1:], F32)
    half = ids.shape[0] // 2
    for k in range(count):
        block = source[pl.ds(ids[first + k], 1), :]
        total = total + weights[ids[half + first + k]] * block
    return jnp.sum(total.T, axis=0, keepdims=True)


def sst_kernel(width, ids, from_west, ocean, mask, weights, sst, window, halves):
    window[:8, :] = from_west[24:32, :]
    window[8:, :] = mask[...].astype(F32) * ocean[:8, :]
    rows = sst.shape[0]

    @pl.loop(0, rows)
    def _(row):
        for g in range(2):
            halves[g, pl.ds(row, 1), :] = mat_vec(ids, (row * 2 + g) * width, width, window, weights)

    for g in range(2):
        sst[:, g * LANES : (g + 1) * LANES] = halves[g]


def solve_kernel(place, columns, inverse, factor, sst, out, flux, held, turned, sems):
    sub = place[0]
    groups, band, depth, cells = columns.shape
    levels = groups * depth
    parts, step = out.shape[1], out.shape[3]
    high, low = split(inverse[sub])
    thrice = jnp.concatenate([high, high, low], axis=1)
    copies = []
    for part in range(parts):
        for row in range(part * step, (part + 1) * step):
            x_high, x_low = split(columns[:, row].reshape(levels, cells))
            held[row] = jnp.dot(
                thrice, jnp.concatenate([x_high, x_low, x_high], axis=0), preferred_element_type=F32
            )
        for group in range(groups):
            turned[group, part] = jnp.swapaxes(
                held[part * step : (part + 1) * step, group * depth : (group + 1) * depth, :], 0, 1
            )
            copies.append(
                pltpu.make_async_copy(
                    turned.at[group, part], out.at[group, part], sems.at[group * parts + part]
                )
            )
            copies[-1].start()
    rows = pl.ds(pl.multiple_of(sub * band, band), band)
    flux[...] = factor[rows, :] * (sst[...] - held[:, levels - 1, :])
    for copy in copies:
        copy.wait()


def ocean_kernel(
    width, n_sub, place, ids, flux, from_east_flux, weights, temp_in, diffusivity, mask_in, inverse,
    from_west, from_east, even_rows, odd_rows, folded, out, window, picked, sems,
):
    sub = place[0]
    band = flux.shape[0]
    entries = picked.shape[0]
    picks = [
        pltpu.make_async_copy(weights.at[ids[entries + i]], picked.at[i], sems.at[i])
        for i in range(entries)
    ]
    for pick in picks:
        pick.start()
    for side, source in enumerate((flux, from_east_flux)):
        for g in range(2):
            at = (side * 2 + g) * band
            window[at : at + band, :] = source[:, g * LANES : (g + 1) * LANES]
    levels, rows, cells = temp_in.shape
    temp = temp_in[...]
    mask = mask_in[...].astype(F32)
    even = lax.rem(sub, 2) == 0
    own_south = temp[:, 0, :]
    south_row = jnp.where(even, jnp.where(sub == 0, own_south, odd_rows[...]), even_rows[...])
    north_row = jnp.where(
        even, even_rows[...], jnp.where(sub == n_sub - 1, folded[...], odd_rows[...])
    )
    south = jnp.concatenate([south_row[:, None, :], temp[:, :-1, :]], axis=1)
    north = jnp.concatenate([temp[:, 1:, :], north_row[:, None, :]], axis=1)

    def column(message):
        side = message[16:24, :].T
        return jnp.concatenate([side[:, 0:1], side[:, 1:2]], axis=0)

    flat = temp.reshape(levels * rows, cells)
    lane = lax.broadcasted_iota(jnp.int32, flat.shape, 1)
    west = jnp.where(lane == 0, column(from_west), pltpu.roll(flat, 1, 1))
    east = jnp.where(lane == cells - 1, column(from_east), pltpu.roll(flat, cells - 1, 1))
    lap = (west + east).reshape(temp.shape) + north + south - 4.0 * temp
    stepped = mask[None] * (temp + diffusivity[...][None] * lap)
    by_row = jnp.swapaxes(stepped, 0, 1)
    level = lax.broadcasted_iota(jnp.int32, (levels, cells), 0)
    high, low = split(inverse[...])
    made = []
    for row in range(rows):
        total = jnp.zeros((LANES, LANES), F32)
        for k in range(row * width, (row + 1) * width):
            picks[k].wait()
            total = total + picked[k] * window[pl.ds(ids[k], 1), :]
        heat = mask[row : row + 1, :] * jnp.sum(total.T, axis=0, keepdims=True)
        x_high, x_low = split(by_row[row] + jnp.where(level == 0, heat, 0.0))
        made.append(
            jnp.dot(high, x_high, preferred_element_type=F32)
            + jnp.dot(high, x_low, preferred_element_type=F32)
            + jnp.dot(low, x_high, preferred_element_type=F32)
        )
    out[...] = jnp.swapaxes(jnp.stack(made), 0, 1)


def place_kernel(parts, out, sems):
    bands, pieces, _, step, _ = parts.shape
    copies = []
    for band in range(bands):
        for piece in range(pieces):
            at = band * pieces + piece
            rows = pl.ds(at * step, step)
            copies.append(pltpu.make_async_copy(parts.at[band, piece], out.at[:, rows, :], sems.at[at]))
            copies[-1].start()
    for copy in copies:
        copy.wait()


def pair_exchanges(n_lon, n_sub):
    first, second = [], []
    for lon in range(n_lon):
        at = lon * n_sub
        for south in range(n_sub - 1):
            pairs = first if south % 2 == 0 else second
            pairs += [(at + south, at + south + 1), (at + south + 1, at + south)]
        second.append((at + n_sub - 1, (n_lon - 1 - lon) * n_sub + n_sub - 1))
    return first, second


def per_device(
    atm_tracer,
    courant,
    column_inverse,
    heat_exchange_factor,
    ocean_temp,
    diffusivity,
    ocean_inverse,
    land_mask,
    weights,
    a2o_src,
    a2o_wgt,
    o2a_src,
    o2a_wgt,
):
    lon_index = lax.axis_index("lon")
    sub_index = lax.axis_index("sub")
    n_lon = lax.axis_size("lon")
    n_sub = lax.axis_size("sub")
    lev_dev, alat, alon_dev = atm_tracer.shape
    groups = alon_dev // LANES
    ngroups = groups * n_lon
    olev, olat_dev, olon_dev = ocean_temp.shape
    aband = alat // n_sub
    width = o2a_src.shape[2]
    ocean_flat = ocean_temp.reshape(olev * olat_dev, olon_dev)
    place = jnp.reshape(sub_index, (1,))

    east_msg, west_msg, even_msg, odd_msg, atm_here = kernel_call(
        edges_kernel,
        (shape(32, LANES), shape(24, LANES), shape(olev, LANES), shape(olev, LANES), in_vmem(lev_dev, alat, alon_dev)),
        [SMEM] + [HBM] * 3, (VMEM,) * 5,
        scratch=[
            pltpu.VMEM(ocean_flat.shape, F32), pltpu.VMEM(land_mask.shape, land_mask.dtype),
            pltpu.SemaphoreType.DMA((PIECES + 2,)),
        ],
        flops=2 * MIB, moved=2 * MIB, name="edges",
    )(place, stays(atm_tracer), stays(ocean_flat), stays(land_mask))
    up = [(i, (i + 1) % n_lon) for i in range(n_lon)]
    down = [(b, a) for a, b in up]
    from_west = lax.ppermute(east_msg, "lon", up)
    from_east = lax.ppermute(west_msg, "lon", down)

    first, second = pair_exchanges(n_lon, n_sub)
    even_rows = lax.ppermute(even_msg, ("lon", "sub"), first)
    odd_rows = lax.ppermute(odd_msg, ("lon", "sub"), second)

    base, west_speed, east_speed = kernel_call(
        base_kernel,
        (in_vmem(n_sub, aband, lev_dev, alon_dev), shape(lev_dev, LANES), shape(lev_dev, LANES)),
        [VMEM] * 2, (VMEM,) * 3, flops=10 * MIB, moved=6 * MIB, name="base",
    )(atm_here, courant)
    advected = kernel_call(
        inflow_kernel, in_hbm(n_sub, aband, lev_dev, alon_dev), [VMEM] * 5, HBM,
        scratch=[pltpu.VMEM((n_sub, aband, lev_dev, alon_dev), F32), pltpu.SemaphoreType.DMA((n_sub,))],
        flops=2 * MIB, moved=4 * MIB, name="inflow",
    )(base, west_speed, east_speed, from_west, from_east)
    columns = lax.all_to_all(advected, "sub", split_axis=0, concat_axis=0, tiled=True)

    band_src = lax.dynamic_slice_in_dim(o2a_src, sub_index * aband, aband, 0).reshape(-1)
    band_wgt = lax.dynamic_slice_in_dim(o2a_wgt, sub_index * aband, aband, 0).reshape(-1)
    tile = jnp.remainder(band_src % n_lon - lon_index + 1, n_lon)
    sea_ids = tile * olat_dev + band_src // n_lon - sub_index * olat_dev
    sst = kernel_call(
        functools.partial(sst_kernel, width), shape(aband, alon_dev), [SMEM] + [VMEM] * 4, VMEM,
        scratch=[pltpu.VMEM((2 * olat_dev, LANES), F32), pltpu.VMEM((groups, aband, LANES), F32)],
        flops=8 * MIB, moved=8 * MIB, name="sst",
    )(jnp.concatenate([sea_ids, band_wgt]), from_west, ocean_flat, land_mask, weights)
    step = 8
    halves = aband // step
    solved, flux_band = kernel_call(
        solve_kernel, (in_hbm(n_sub, halves, lev_dev, step, alon_dev), shape(aband, alon_dev)),
        [SMEM] + [VMEM] * 4, (HBM, VMEM),
        scratch=[
            pltpu.VMEM((aband, lev_dev * n_sub, alon_dev), F32),
            pltpu.VMEM((n_sub, halves, lev_dev, step, alon_dev), F32), pltpu.SemaphoreType.DMA((n_sub * halves,)),
        ],
        flops=400 * MIB, moved=4 * MIB, name="solve",
    )(place, columns, column_inverse, heat_exchange_factor, sst)
    solved, even_rows, odd_rows = lax.optimization_barrier((solved, even_rows, odd_rows))
    folded = jnp.flip(odd_rows, axis=1)
    parts = lax.all_to_all(solved, "sub", split_axis=0, concat_axis=0, tiled=True)
    east_flux = lax.ppermute(flux_band, "lon", down)

    src = a2o_src.reshape(-1)
    group = jnp.remainder(src % ngroups - lon_index * groups, ngroups)
    flux_ids = group * aband + src // ngroups - sub_index * aband
    entries = src.shape[0]
    ocean_new = kernel_call(
        functools.partial(ocean_kernel, width, n_sub), shape(olev, olat_dev, olon_dev),
        [SMEM] * 2 + [VMEM] * 2 + [HBM] + [VMEM] * 9, VMEM,
        scratch=[
            pltpu.VMEM((4 * aband, LANES), F32), pltpu.VMEM((entries, LANES, LANES), F32),
            pltpu.SemaphoreType.DMA((entries,)),
        ],
        flops=8 * MIB, moved=4 * MIB, name="ocean",
    )(
        place, jnp.concatenate([flux_ids, a2o_wgt.reshape(-1)]), flux_band, east_flux, stays(weights),
        ocean_temp, diffusivity, land_mask, ocean_inverse, from_west, from_east, even_rows, odd_rows, folded,
    )
    returned = kernel_call(
        place_kernel, shape(lev_dev, alat, alon_dev), [VMEM], HBM,
        scratch=[pltpu.SemaphoreType.DMA((n_sub * halves,))], moved=4 * MIB, name="place",
    )(parts)
    return returned, ocean_new, flux_band


def solution(mesh):
    return jax.shard_map(
        per_device,
        mesh=mesh,
        in_specs=(
            P("sub", None, "lon"),
            P("sub", None, "lon"),
            P(),
            P(None, "lon"),
            P(None, "sub", "lon"),
            P("sub", "lon"),
            P(),
            P("sub", "lon"),
            P(),
            P("sub", "lon", None),
            P("sub", "lon", None),
            P(None, "lon", None),
            P(None, "lon", None),
        ),
        out_specs=(P("sub", None, "lon"), P(None, "sub", "lon"), P("sub", "lon")),
        check_vma=False,
    )
```
